32 devices in a mesh: band: 2 (over x), chan: 8 (over z, y), pair: 2 (over core).
Axes of the slice: x: 2, y: 2, z: 4, core: 2. Of those that a mesh axis runs over, the one named last changes fastest.
Arguments:
- samples: int32 [2, 2048, 32768], P(None, 'chan', ('band', 'pair')), parts along dimension 2, may hold values from -8 to 6, as said below
- taps: int32 [4, 1024], replicated, may hold values from -127 to 127
- tile_order: int32 [36], replicated, may hold values from 0 to 35, each once
Outputs:
- visibilities: bfloat16 [16, 36, 2, 256, 256], P(('band', 'chan'), 'pair'), parts along dimension 0
The draws below stay inside these ranges and needn't reach their ends.
There are 2 independent parts, one for each index of `band`. The reference program is written for one: setup_inputs(seed, part) draws one part's arguments, and reference() takes and returns one part's arrays. A program takes and returns all parts, laid end to end along the dimension named above; an argument that names none is the same for every part. Nothing has to cross between parts.
Inputs may be any that keep to these rules, and one draw needn't show every extreme that they name: 4-bit voltage samples with a component common to all inputs.
All inputs are finite; a program needn't handle non-finite values.
Results may differ from the reference program's by a relative error of at most 0.0034.
Values may be sent and summed in bfloat16 or wider, within the bound.
No kernel may reach another device: no remote copies, remote signals or barrier semaphores. Data moves between devices by JAX's collectives and lax.ppermute only.
A program may use at most 320 MiB of HBM per device.

```python
import math
import jax
import jax.numpy as jnp
import numpy as np
from jax import lax

INPUTS = 2048
NFFT = 1024
TAPS = 4
BLOCK = 256
FRAMES = 16
SAMPLES = 16384
AVG = 128
GROUPS = 8
NB = 8
NPAIRS = 36


def draw_samples(key, part):
    key = jax.random.fold_in(key, 5)
    shared = jax.random.randint(jax.random.fold_in(key, 11), (2, 1, SAMPLES), -2, 2)
    own = jax.random.randint(jax.random.fold_in(key, 12), (2, INPUTS, SAMPLES), -6, 6)
    return (own + shared).astype(jnp.int32)


def place_ends(values, rng, smallest, high):
    extent = values.shape
    index_at = [jax.random.randint(jax.random.fold_in(rng, axis), (), 0, extent[axis]) for axis in range(len(extent))]
    values = values.at[tuple(index_at)].set(smallest)
    longest = extent.index(max(extent))
    index_at[longest] = (index_at[longest] + 1) % extent[longest]
    return values.at[tuple(index_at)].set(high)


def setup_inputs(seed: int = 0, part: int = 0) -> dict:
    streams_of = jax.random.split(jax.random.key(seed), 4)
    part_splits = jax.random.split(jax.random.fold_in(streams_of[3], part), 4)
    samples = draw_samples(jax.random.fold_in(jax.random.fold_in(streams_of[3], part), 71), part)
    taps = place_ends(jax.random.randint(streams_of[1], (TAPS, NFFT), -127, 128), jax.random.fold_in(streams_of[1], 1), -127, 127).astype(jnp.int32)
    tile_order = jax.random.permutation(streams_of[2], NPAIRS).astype(jnp.int32)
    return {"samples": samples, "taps": taps, "tile_order": tile_order}


def dft_table(length):
    index = jnp.arange(length, dtype=jnp.int32)
    phase = (index[:, None] * index[None, :]) % length
    angle = phase.astype(jnp.float32) * (2.0 * math.pi / length)
    cosine = jnp.cos(angle)
    sine = jnp.sin(angle)
    upper = jnp.stack([cosine, -sine], axis=1)
    lower = jnp.stack([sine, cosine], axis=1)
    return jnp.concatenate([upper, lower], axis=0).astype(jnp.bfloat16)


def reference(samples, taps, tile_order):
    zeros = jnp.zeros((2, INPUTS, (TAPS - 1) * NFFT), jnp.float32)
    longer = jnp.concatenate([zeros, samples.astype(jnp.float32)], axis=2)
    framed = longer.reshape(2, INPUTS, FRAMES + TAPS - 1, NFFT)
    weights = taps.astype(jnp.float32)
    filtered = jnp.zeros((2, INPUTS, FRAMES, NFFT), jnp.float32)
    for tap_index in range(TAPS):
        filtered = filtered + weights[tap_index][None, None, None, :] * framed[:, :, tap_index:tap_index + FRAMES, :]
    filtered = filtered.astype(jnp.bfloat16)
    left = jnp.concatenate([filtered[0], filtered[1]], axis=-1).reshape(INPUTS * FRAMES, 2 * NFFT)
    table = dft_table(NFFT).reshape(2 * NFFT, 2 * NFFT)
    product = jnp.dot(left.astype(jnp.float32), table.astype(jnp.float32), precision=lax.Precision.HIGHEST)
    spectra = (product * (2.0 ** -14)).astype(jnp.bfloat16).reshape(INPUTS, FRAMES, 2, NFFT)
    spectra = jnp.transpose(spectra, (0, 2, 3, 1)).reshape(INPUTS, 2, GROUPS, AVG * FRAMES)
    spectra = jnp.moveaxis(spectra, 2, 0)
    rows_np, cols_np = np.triu_indices(NB)
    first = jnp.asarray(rows_np.astype(np.int32))[tile_order]
    second = jnp.asarray(cols_np.astype(np.int32))[tile_order]
    factor = 1.0 / (FRAMES * AVG)

    def correlate(group_data):
        blocks = group_data.astype(jnp.float32).reshape(NB, BLOCK, 2, AVG * FRAMES)
        left_blocks = blocks[first]
        right_blocks = blocks[second]
        real = jnp.einsum('suck,svck->suv', left_blocks, right_blocks, precision=lax.Precision.HIGHEST)
        imag = jnp.einsum('suk,svk->suv', left_blocks[:, :, 1], right_blocks[:, :, 0], precision=lax.Precision.HIGHEST)
        imag = imag - jnp.einsum('suk,svk->suv', left_blocks[:, :, 0], right_blocks[:, :, 1], precision=lax.Precision.HIGHEST)
        return (jnp.stack([real, imag], axis=1) * factor).astype(jnp.bfloat16)

    return lax.map(correlate, spectra)
```

```python
import functools
import math

import jax
import jax.numpy as jnp
import ml_dtypes
import numpy as np
from jax import lax
from jax.experimental import pallas as pl
from jax.experimental.pallas import tpu as pltpu
from jax.sharding import PartitionSpec as P

BLOCK = 256
UNROLL = 3
COST = 10**11
LANES = 128
ROWS = 32
SCALE = 2.0**-14
VMEM_LIMIT = 56 * 1024 * 1024

PLAN = (2, 3, 3)


def passed_along(block, axis, distance):
    devices = range(lax.axis_size(axis))
    route = [(i - distance, i) for i in devices if i - distance in devices]
    return lax.ppermute(block, axis, route)


def swapped_with(block, axis, mask):
    return lax.ppermute(block, axis, [(i, i ^ mask) for i in range(lax.axis_size(axis))])


def grouped_table(length, groups):
    index = np.arange(length)
    angle = (index[:, None] * index[None, :] % length).astype(np.float32) * np.float32(2.0 * math.pi / length)
    cosine = np.cos(angle).astype(ml_dtypes.bfloat16).astype(np.float32) * SCALE
    sine = np.sin(angle).astype(ml_dtypes.bfloat16).astype(np.float32) * SCALE
    both = np.stack([cosine, sine], axis=1).reshape(length, 2, groups, length // groups)
    return both.transpose(2, 0, 1, 3).reshape(groups, length, 2 * (length // groups)).astype(ml_dtypes.bfloat16)


def front_kernel(geometry, samples, *refs):
    first, count, sends, with_rim, gated, fft_size, tap_count = geometry
    groups = len(sends)
    reach = tap_count - 1
    early = max(0, reach - first)
    own = count + reach - early
    refs = list(refs)
    rim_in = refs.pop(0) if early else None
    taps, table = refs.pop(0), refs.pop(0)
    if gated:
        refs.pop(0)
    pieces = [[refs.pop(0) for _ in widths] for widths in sends[: groups // 2]]
    near_out = refs.pop(0) if sends[-1] else None
    for j in range(groups // 2, groups):
        pieces.append([near_out.at[j - groups // 2]] if near_out is not None else [])
    rim_out = refs.pop(0) if with_rim else None
    held = refs.pop(0)
    held_rim = refs.pop(0) if early else None
    tables, left, results = refs.pop(0), refs.pop(0), refs.pop(0)
    rim_made = refs.pop(0) if with_rim else None
    in_sems, table_sems, out_sems = refs[:3]
    steps = BLOCK // ROWS
    me = lax.axis_index("chan")

    def copies_in(step):
        rows = pl.ds(pl.multiple_of(step * ROWS, ROWS), ROWS)
        lanes = pl.ds((first - reach + early) * fft_size, own * fft_size)
        made = [pltpu.make_async_copy(samples.at[:, rows, lanes], held.at[:, rows, :], in_sems.at[0, step])]
        if early:
            lanes = pl.ds((reach - early) * fft_size, early * fft_size)
            made.append(pltpu.make_async_copy(rim_in.at[:, rows, lanes], held_rim.at[:, rows, :], in_sems.at[1, step]))
        return made

    def copy_table(j):
        group = me ^ (j + groups // 2) if j < groups // 2 else me - lax.rem(me, groups // 2) + (j - groups // 2)
        return pltpu.make_async_copy(table.at[group], tables.at[j], table_sems.at[j])

    def copies_out(j):
        made, f = [], 0
        for w, width in enumerate(sends[j]):
            part = results.at[j, :, f * BLOCK : (f + width) * BLOCK]
            made.append(pltpu.make_async_copy(part, pieces[j][w], out_sems.at[j, w]))
            f += width
        return made

    used = [j for j in range(groups) if sends[j]]
    for step in range(steps):
        for copy in copies_in(step):
            copy.start()
    for j in used:
        copy_table(j).start()

    def filter_rows(step, carry):
        for copy in copies_in(step):
            copy.wait()
        rows = pl.ds(pl.multiple_of(step * ROWS, ROWS), ROWS)
        for part in range(2):
            for start in range(0, fft_size, LANES):
                values = []
                for k in range(early):
                    lanes = slice(k * fft_size + start, k * fft_size + start + LANES)
                    values.append(held_rim[part, rows, lanes].astype(jnp.float32))
                for k in range(own):
                    lanes = slice(k * fft_size + start, k * fft_size + start + LANES)
                    values.append(held[part, rows, lanes].astype(jnp.float32))
                lanes = slice(start, start + LANES)
                weights = [taps[t : t + 1, lanes].astype(jnp.float32) for t in range(tap_count)]
                for f in range(count):
                    total = weights[0] * values[f]
                    for t in range(1, tap_count):
                        total = total + weights[t] * values[f + t]
                    at = pl.ds(pl.multiple_of(f * BLOCK + step * ROWS, ROWS), ROWS)
                    left[part, at, lanes] = total.astype(jnp.bfloat16)
                if with_rim:
                    for t in range(reach):
                        lanes = slice(t * fft_size + start, t * fft_size + start + LANES)
                        rim_made[part, rows, lanes] = values[count + t].astype(jnp.bfloat16)
        return carry

    lax.fori_loop(0, steps, filter_rows, 0)
    if with_rim:
        rim_copy = pltpu.make_async_copy(rim_made, rim_out, in_sems.at[1, 0])
        rim_copy.start()

    def transform(j, frames):
        pltpu.make_async_copy(table.at[0], tables.at[j], table_sems.at[j]).wait()
        rows = frames * BLOCK
        product = [
            jnp.dot(left[part, :rows, :], tables[j], preferred_element_type=jnp.float32) for part in range(2)
        ]
        real = (product[0][:, :LANES] + product[1][:, LANES:]).astype(jnp.bfloat16)
        imag = (product[1][:, :LANES] - product[0][:, LANES:]).astype(jnp.bfloat16)
        for f in range(frames):
            results[j, :, f * BLOCK : f * BLOCK + LANES] = real[f * BLOCK : (f + 1) * BLOCK]
            results[j, :, f * BLOCK + LANES : (f + 1) * BLOCK] = imag[f * BLOCK : (f + 1) * BLOCK]
        for k in used:

            @pl.when(j == k)
            def _():
                for copy in copies_out(k):
                    copy.start()

    begin = 0
    while begin < len(used):
        end = begin
        while end < len(used) and sum(sends[end]) == sum(sends[begin]):
            end += 1

        def several(j, carry, frames=sum(sends[begin])):
            transform(j, frames)
            return carry

        lax.fori_loop(begin, end, several, 0, unroll=2)
        begin = end
    if with_rim:
        rim_copy.wait()
    for j in used:
        for copy in copies_out(j):
            copy.wait()


def front(samples, rim, taps, table, gate, first, count, sends, with_rim):
    fft_size = taps.shape[1]
    tap_count = taps.shape[0]
    reach = tap_count - 1
    groups, depth, columns = len(sends), table.shape[1], table.shape[2]
    early = max(0, reach - first)
    own = count + reach - early
    anywhere = pl.BlockSpec(memory_space=pl.ANY)
    vmem = pl.BlockSpec(memory_space=pltpu.VMEM)
    operands = [samples] + ([rim] if early else []) + [taps, table] + ([] if gate is None else [gate])
    in_specs = [anywhere] + ([anywhere] if early else []) + [vmem, anywhere] + ([] if gate is None else [anywhere])
    out_shape = []
    for widths in sends[: groups // 2]:
        for width in widths:
            out_shape.append(jax.ShapeDtypeStruct((BLOCK, width * columns), jnp.bfloat16))
    if sends[-1]:
        out_shape.append(jax.ShapeDtypeStruct((groups // 2, BLOCK, sends[-1][0] * columns), jnp.bfloat16))
    scratch = [pltpu.VMEM((2, BLOCK, own * fft_size), jnp.int32)]
    if early:
        scratch.append(pltpu.VMEM((2, BLOCK, early * fft_size), jnp.bfloat16))
    scratch += [
        pltpu.VMEM((groups, depth, columns), jnp.bfloat16),
        pltpu.VMEM((2, count * BLOCK, depth), jnp.bfloat16),
        pltpu.VMEM((groups, BLOCK, count * columns), jnp.bfloat16),
    ]
    if with_rim:
        out_shape.append(jax.ShapeDtypeStruct((2, BLOCK, reach * fft_size), jnp.bfloat16))
        scratch.append(pltpu.VMEM((2, BLOCK, reach * fft_size), jnp.bfloat16))
    scratch += [
        pltpu.SemaphoreType.DMA((2, BLOCK // ROWS)),
        pltpu.SemaphoreType.DMA((groups,)),
        pltpu.SemaphoreType.DMA((groups, max(len(widths) for widths in sends))),
    ]
    geometry = (first, count, sends, with_rim, gate is not None, fft_size, tap_count)
    results = list(
        pl.pallas_call(
            functools.partial(front_kernel, geometry),
            in_specs=in_specs,
            out_specs=[anywhere] * len(out_shape),
            out_shape=out_shape,
            scratch_shapes=scratch,
            compiler_params=pltpu.CompilerParams(vmem_limit_bytes=VMEM_LIMIT),
            cost_estimate=pl.CostEstimate(flops=COST, bytes_accessed=1, transcendentals=0),
        )(*operands)
    )
    pieces = [[results.pop(0) for _ in widths] for widths in sends[: groups // 2]]
    return pieces, results[0] if with_rim or sends[-1] else None


def gather_kernel(layout, *refs):
    parts, out, held, in_sems, out_sems = refs[:-4], *refs[-4:]
    copies, sends = [], []
    for d, places in enumerate(layout):
        f = 0
        for w, (number, at, start, width) in enumerate(places):
            source = parts[number] if at is None else parts[number].at[at]
            source = source.at[:, start * BLOCK : (start + width) * BLOCK]
            target = held.at[d, :, f * BLOCK : (f + width) * BLOCK]
            copies.append((d, pltpu.make_async_copy(source, target, in_sems.at[d, w])))
            f += width
        sends.append(pltpu.make_async_copy(held.at[d], out.at[d], out_sems.at[d]))
    for _, copy in copies:
        copy.start()
    for d, send in enumerate(sends):
        for owner, copy in copies:
            if owner == d:
                copy.wait()
        send.start()
    for send in sends:
        send.wait()


def gathered(blocks, after):
    operands, layout = [], []
    for block in blocks:
        places = []
        for array, at, start, width in block:
            places.append((len(operands), at, start, width))
            operands.append(array)
        layout.append(tuple(places))
    frames = sum(place[3] for place in layout[0])
    shape = (len(blocks), BLOCK, frames * BLOCK)
    operands += [] if after is None else [after]
    return pl.pallas_call(
        functools.partial(gather_kernel, tuple(layout)),
        in_specs=[pl.BlockSpec(memory_space=pl.ANY)] * len(operands),
        out_specs=pl.BlockSpec(memory_space=pl.ANY),
        out_shape=jax.ShapeDtypeStruct(shape, jnp.bfloat16),
        scratch_shapes=[
            pltpu.VMEM(shape, jnp.bfloat16),
            pltpu.SemaphoreType.DMA((len(blocks), max(len(places) for places in layout))),
            pltpu.SemaphoreType.DMA((len(blocks),)),
        ],
        compiler_params=pltpu.CompilerParams(vmem_limit_bytes=VMEM_LIMIT),
        cost_estimate=pl.CostEstimate(flops=1, bytes_accessed=1, transcendentals=0),
    )(*operands)


def tile_kernel(geometry, first, second, *refs):
    count, has_sums, factor = geometry
    blocks = refs[:count]
    sums = refs[count] if has_sums else None
    refs = refs[count + has_sums :]
    out, held, totals = refs[0], refs[1 : 1 + count], refs[1 + count]
    finished = refs[2 + count]
    block_sems, sum_sems, out_sems = refs[-3:]
    slots = totals.shape[0]
    numbers = blocks[0].shape[0]
    block_copies = [
        pltpu.make_async_copy(blocks[k].at[d], held[k].at[d], block_sems.at[k, d])
        for d in range(numbers)
        for k in range(count)
    ]
    for copy in block_copies:
        copy.start()

    def copy_in(slot):
        return pltpu.make_async_copy(sums.at[slot], totals.at[slot], sum_sems.at[slot])

    def copy_out(slot):
        return pltpu.make_async_copy(finished.at[slot], out.at[slot], out_sems.at[slot])

    if has_sums:
        for slot in range(slots):
            copy_in(slot).start()
    for copy in block_copies:
        copy.wait()
    if has_sums:
        for slot in range(slots):
            copy_in(slot).wait()

    def correlate(slot, carry):
        a, b = first[slot], second[slot]
        total = None
        for block in held:
            left, right = block[a], block[b]
            turned = []
            for start in range(0, left.shape[1], 2 * LANES):
                turned += [left[:, start + LANES : start + 2 * LANES], -left[:, start : start + LANES]]
            both = jnp.concatenate([left, jnp.concatenate(turned, axis=1)], axis=0)
            term = lax.dot_general(both, right, (((1,), (1,)), ((), ())), preferred_element_type=jnp.float32)
            total = term if total is None else total + term
        if has_sums:
            total = total + totals[slot]
        if factor is not None:
            total = total * factor
        finished[slot] = total.astype(finished.dtype)
        copy_out(slot).start()
        return carry

    lax.fori_loop(0, slots, correlate, 0, unroll=UNROLL)
    for slot in range(slots):
        copy_out(slot).wait()


def tiles(first, second, blocks, sums, factor):
    slots = first.shape[0]
    anywhere = pl.BlockSpec(memory_space=pl.ANY)
    smem = pl.BlockSpec(memory_space=pltpu.SMEM)
    operands = list(blocks) + ([] if sums is None else [sums])
    width = sum(block.shape[2] for block in blocks)
    shape = (slots, 2 * BLOCK, BLOCK)
    kind = jnp.float32 if factor is None else jnp.bfloat16
    scratch = [pltpu.VMEM(block.shape, block.dtype) for block in blocks] + [pltpu.VMEM(shape, jnp.float32), pltpu.VMEM(shape, kind)]
    scratch += [
        pltpu.SemaphoreType.DMA((len(blocks), blocks[0].shape[0])),
        pltpu.SemaphoreType.DMA((slots,)),
        pltpu.SemaphoreType.DMA((slots,)),
    ]
    return pl.pallas_call(
        functools.partial(tile_kernel, (len(blocks), sums is not None, factor)),
        in_specs=[smem, smem] + [anywhere] * len(operands),
        out_specs=anywhere,
        out_shape=jax.ShapeDtypeStruct(shape, kind),
        scratch_shapes=scratch,
        compiler_params=pltpu.CompilerParams(vmem_limit_bytes=VMEM_LIMIT),
        cost_estimate=pl.CostEstimate(flops=COST, bytes_accessed=1, transcendentals=0),
    )(first, second, *operands)


def dft_table(length):
    index = jnp.arange(length, dtype=jnp.int32)
    phase = index[:, None] * index[None, :] % length
    angle = phase.astype(jnp.float32) * (2.0 * math.pi / length)
    cosine = jnp.cos(angle)
    sine = jnp.sin(angle)
    upper = jnp.stack([cosine, -sine], axis=1)
    lower = jnp.stack([sine, cosine], axis=1)
    return jnp.concatenate([upper, lower], axis=0).astype(jnp.bfloat16)


def tile_products(spectra, slots, tile_count):
    input_count = spectra.shape[0]
    block_count = input_count // BLOCK
    width = spectra.shape[1] * spectra.shape[2] * spectra.shape[3]
    rows_np, cols_np = np.triu_indices(block_count)
    numbers = jnp.arange(tile_count, dtype=jnp.int32)
    match = (slots[:, None] == numbers[None, :]).astype(jnp.int32)
    first = jnp.sum(match * jnp.asarray(rows_np.astype(np.int32))[None, :], axis=1)
    second = jnp.sum(match * jnp.asarray(cols_np.astype(np.int32))[None, :], axis=1)
    swapped = jnp.stack([spectra[:, :, 1], -spectra[:, :, 0]], axis=2)
    plain_blocks = spectra.reshape(block_count, BLOCK, width)
    paired = jnp.stack([plain_blocks, swapped.reshape(block_count, BLOCK, width)], axis=1)
    left_blocks = paired[first]
    right_blocks = plain_blocks[second]
    return jnp.einsum(
        "scuw,svw->scuv", left_blocks, right_blocks, preferred_element_type=jnp.float32
    )


def any_sizes(samples, taps, tile_order):
    inputs_here = samples.shape[1]
    sample_count = samples.shape[2]
    tap_count = taps.shape[0]
    fft_size = taps.shape[1]
    frame_count = sample_count // fft_size
    volts = samples.astype(jnp.bfloat16)
    rim_length = (tap_count - 1) * fft_size
    earlier = passed_along(volts[:, :, sample_count - rim_length :], "pair", 1)
    longer = jnp.concatenate([earlier, volts], axis=2).astype(jnp.float32)
    framed = longer.reshape(2, inputs_here, frame_count + tap_count - 1, fft_size)
    weights = taps.astype(jnp.float32)
    filtered = jnp.zeros((2, inputs_here, frame_count, fft_size), jnp.float32)
    for tap_index in range(tap_count):
        filtered = (
            filtered
            + weights[tap_index][None, None, None, :]
            * framed[:, :, tap_index : tap_index + frame_count, :]
        )
    filtered = filtered.astype(jnp.bfloat16)
    left = jnp.concatenate([filtered[0], filtered[1]], axis=-1)
    table = dft_table(fft_size)
    spectra = jnp.einsum("xfm,mck->xfck", left, table, preferred_element_type=jnp.float32)
    chan_size = lax.axis_size("chan")
    group_width = fft_size // chan_size
    spectra = (
        (spectra * 2.0 ** (-14))
        .astype(jnp.bfloat16)
        .reshape(inputs_here, frame_count, 2, chan_size, group_width)
    )
    turned = lax.all_to_all(spectra, "chan", split_axis=3, concat_axis=0, tiled=True)
    turned = turned.reshape(turned.shape[0], frame_count, 2, group_width)
    tile_count = tile_order.shape[0]
    pair_size = lax.axis_size("pair")
    factor = 1.0 / (frame_count * group_width * pair_size)
    summed = lax.psum_scatter(
        tile_products(turned, tile_order, tile_count), "pair", scatter_dimension=0, tiled=True
    )
    return (summed * factor).astype(jnp.bfloat16)[None]


def per_device(samples, taps, tile_order):
    fft_size = taps.shape[1]
    groups = lax.axis_size("chan")
    pair_size = lax.axis_size("pair")
    me = lax.axis_index("chan").astype(jnp.int32)
    far = groups // 2
    table = jnp.asarray(grouped_table(fft_size, groups))

    slots = tile_order.shape[0] // pair_size
    own_slots = lax.dynamic_slice(tile_order, (lax.axis_index("pair") * slots,), (slots,))
    rows_np, cols_np = np.triu_indices(groups)
    match = (own_slots[:, None] == jnp.arange(tile_order.shape[0], dtype=jnp.int32)[None, :]).astype(jnp.int32)

    def place_of(blocks_np):
        block = jnp.sum(match * jnp.asarray(blocks_np.astype(np.int32))[None, :], axis=1)
        return jnp.where(block // far == me // far, block % far, block ^ me)

    first, second = place_of(rows_np), place_of(cols_np)

    def after(value, *others):
        return lax.optimization_barrier((value, *others))[0]

    def to(mask, value):
        return swapped_with(value, "chan", mask)

    def other_core(value):
        return swapped_with(value, "pair", 1)

    def among_near(value):
        halves = [list(range(start, start + far)) for start in range(0, groups, far)]
        return lax.all_to_all(value, "chan", 0, 0, axis_index_groups=halves, tiled=True)

    apart = range(far, groups)
    FIRST, SECOND, THIRD = PLAN
    end = samples.shape[2] // fft_size
    start_a, start_b = end - FIRST, end - FIRST - SECOND
    made_a, rim_here = front(samples, None, taps, table, None, start_a, FIRST, ((FIRST,),) * far + ((),) * far, True)
    a = {mask: to(mask, made_a[mask - far][0]) for mask in apart}
    rim = passed_along(rim_here, "pair", 1)
    sends = ((SECOND,),) * far + ((SECOND + FIRST,),) * far
    made_b, near_b = front(samples, None, taps, table, made_a[0][0], start_b, SECOND + FIRST, sends, False)
    b = {mask: to(mask, after(made_b[mask - far][0], a[mask])) for mask in apart}
    ab = among_near(near_b)
    sends = ((THIRD,),) * far + ((THIRD,),) * far
    made_c, near_c = front(samples, rim, taps, table, made_b[0][0], 0, THIRD, sends, False)
    c = {}
    for mask, gates in zip(apart, [(rim,), (b[far], ab)] + [(b[mask],) for mask in apart][1:]):
        c[mask] = to(mask, after(made_c[mask - far][0], *gates))
    cc = among_near(near_c)
    blocks = [[(ab, k, 0, SECOND + FIRST)] for k in range(far)]
    blocks += [[(b[mask], None, 0, SECOND), (a[mask], None, 0, FIRST)] for mask in apart]
    mine = gathered(blocks, None)
    other = other_core(mine)
    sums = tiles(first, second, [mine], None, None)
    sums = tiles(first, second, [other], sums, None)
    blocks = [[(cc, k, 0, THIRD)] for k in range(far)] + [[(c[mask], None, 0, THIRD)] for mask in apart]
    mine = gathered(blocks, sums)
    other = other_core(mine)
    sums = tiles(first, second, [mine], sums, None)
    factor = 1.0 / (end * pair_size * (fft_size // groups))
    sums = tiles(first, second, [other], sums, factor)
    return sums.reshape(1, slots, 2, BLOCK, BLOCK)


def chosen(samples, taps, tile_order):
    groups, pair_size = lax.axis_size("chan"), lax.axis_size("pair")
    whole_blocks = samples.shape[1] == BLOCK and taps.shape[1] == groups * LANES
    halves = groups >= 2 and groups & (groups - 1) == 0 and pair_size == 2
    planned = samples.shape[2] == sum(PLAN) * taps.shape[1] and taps.shape[0] - 1 <= PLAN[2]
    if whole_blocks and halves and planned:
        return per_device(samples, taps, tile_order)
    return any_sizes(samples, taps, tile_order)


def solution(mesh):
    in_specs = (P(None, "chan", ("band", "pair")), P(), P())
    out_specs = P(("band", "chan"), "pair", None, None, None)
    return jax.shard_map(chosen, mesh=mesh, in_specs=in_specs, out_specs=out_specs, check_vma=False)
```

```python
import functools
import math

import jax
import jax.numpy as jnp
import ml_dtypes
import numpy as np
from jax import lax
from jax.experimental import pallas as pl
from jax.experimental.pallas import tpu as pltpu
from jax.sharding import PartitionSpec as P

BLOCK = 256
UNROLL = 3
COST = 10**11
LANES = 128
ROWS = 32
SCALE = 2.0**-14
VMEM_LIMIT = 60 * 1024 * 1024

PLAN = (2, 3, 3)


def passed_along(block, axis, distance):
    devices = range(lax.axis_size(axis))
    route = [(i - distance, i) for i in devices if i - distance in devices]
    return lax.ppermute(block, axis, route)


def swapped_with(block, axis, mask):
    return lax.ppermute(block, axis, [(i, i ^ mask) for i in range(lax.axis_size(axis))])


def grouped_table(length, groups):
    index = np.arange(length)
    angle = (index[:, None] * index[None, :] % length).astype(np.float32) * np.float32(2.0 * math.pi / length)
    cosine = np.cos(angle).astype(ml_dtypes.bfloat16).astype(np.float32) * SCALE
    sine = np.sin(angle).astype(ml_dtypes.bfloat16).astype(np.float32) * SCALE
    both = np.stack([cosine, sine], axis=1).reshape(length, 2, groups, length // groups)
    return both.transpose(2, 0, 1, 3).reshape(groups, length, 2 * (length // groups)).astype(ml_dtypes.bfloat16)


def front_kernel(geometry, samples, *refs):
    first, count, sends, with_rim, gated, fft_size, tap_count = geometry
    groups = len(sends)
    reach = tap_count - 1
    early = max(0, reach - first)
    own = count + reach - early
    refs = list(refs)
    rim_in = refs.pop(0) if early else None
    taps, table = refs.pop(0), refs.pop(0)
    if gated:
        refs.pop(0)
    pieces = [[refs.pop(0) for _ in widths] for widths in sends[: groups // 2]]
    near_out = [refs.pop(0) for _ in sends[-1]]
    for j in range(groups // 2, groups):
        pieces.append([out.at[j - groups // 2] for out in near_out])
    rim_out = refs.pop(0) if with_rim else None
    held = refs.pop(0)
    held_rim = refs.pop(0) if early else None
    tables, left, results = refs.pop(0), refs.pop(0), refs.pop(0)
    rim_made = refs.pop(0) if with_rim else None
    in_sems, table_sems, out_sems = refs[:3]
    steps = BLOCK // ROWS
    me = lax.axis_index("chan")

    def copies_in(step):
        rows = pl.ds(pl.multiple_of(step * ROWS, ROWS), ROWS)
        lanes = pl.ds((first - reach + early) * fft_size, own * fft_size)
        made = [pltpu.make_async_copy(samples.at[:, rows, lanes], held.at[:, rows, :], in_sems.at[0, step])]
        if early:
            lanes = pl.ds((reach - early) * fft_size, early * fft_size)
            made.append(pltpu.make_async_copy(rim_in.at[:, rows, lanes], held_rim.at[:, rows, :], in_sems.at[1, step]))
        return made

    def copy_table(j):
        group = me ^ (j + groups // 2) if j < groups // 2 else me - lax.rem(me, groups // 2) + (j - groups // 2)
        return pltpu.make_async_copy(table.at[group], tables.at[j], table_sems.at[j])

    def copies_out(j):
        made, f = [], 0
        for w, width in enumerate(sends[j]):
            part = results.at[j, :, f * BLOCK : (f + width) * BLOCK]
            made.append(pltpu.make_async_copy(part, pieces[j][w], out_sems.at[j, w]))
            f += width
        return made

    used = [j for j in range(groups) if sends[j]]
    for step in range(steps):
        for copy in copies_in(step):
            copy.start()
    for j in used:
        copy_table(j).start()

    def filter_rows(step, carry):
        for copy in copies_in(step):
            copy.wait()
        rows = pl.ds(pl.multiple_of(step * ROWS, ROWS), ROWS)
        for part in range(2):
            for start in range(0, fft_size, LANES):
                values = []
                for k in range(early):
                    lanes = slice(k * fft_size + start, k * fft_size + start + LANES)
                    values.append(held_rim[part, rows, lanes].astype(jnp.float32))
                for k in range(own):
                    lanes = slice(k * fft_size + start, k * fft_size + start + LANES)
                    values.append(held[part, rows, lanes].astype(jnp.float32))
                lanes = slice(start, start + LANES)
                weights = [taps[t : t + 1, lanes].astype(jnp.float32) for t in range(tap_count)]
                for f in range(count):
                    total = weights[0] * values[f]
                    for t in range(1, tap_count):
                        total = total + weights[t] * values[f + t]
                    at = pl.ds(pl.multiple_of(f * BLOCK + step * ROWS, ROWS), ROWS)
                    left[part, at, lanes] = total.astype(jnp.bfloat16)
                if with_rim:
                    for t in range(reach):
                        lanes = slice(t * fft_size + start, t * fft_size + start + LANES)
                        rim_made[part, rows, lanes] = values[count + t].astype(jnp.bfloat16)
        return carry

    lax.fori_loop(0, steps, filter_rows, 0)
    if with_rim:
        rim_copy = pltpu.make_async_copy(rim_made, rim_out, in_sems.at[1, 0])
        rim_copy.start()

    def transform(j, frames):
        pltpu.make_async_copy(table.at[0], tables.at[j], table_sems.at[j]).wait()
        rows = frames * BLOCK
        product = [
            jnp.dot(left[part, :rows, :], tables[j], preferred_element_type=jnp.float32) for part in range(2)
        ]
        real = (product[0][:, :LANES] + product[1][:, LANES:]).astype(jnp.bfloat16)
        imag = (product[1][:, :LANES] - product[0][:, LANES:]).astype(jnp.bfloat16)
        for f in range(frames):
            results[j, :, f * BLOCK : f * BLOCK + LANES] = real[f * BLOCK : (f + 1) * BLOCK]
            results[j, :, f * BLOCK + LANES : (f + 1) * BLOCK] = imag[f * BLOCK : (f + 1) * BLOCK]
        for k in used:

            @pl.when(j == k)
            def _():
                for copy in copies_out(k):
                    copy.start()

    begin = 0
    while begin < len(used):
        end = begin
        while end < len(used) and sum(sends[end]) == sum(sends[begin]):
            end += 1

        def several(j, carry, frames=sum(sends[begin])):
            transform(j, frames)
            return carry

        lax.fori_loop(begin, end, several, 0, unroll=2)
        begin = end
    if with_rim:
        rim_copy.wait()
    for j in used:
        for copy in copies_out(j):
            copy.wait()


def front(samples, rim, taps, table, gate, first, count, sends, with_rim):
    fft_size = taps.shape[1]
    tap_count = taps.shape[0]
    reach = tap_count - 1
    groups, depth, columns = len(sends), table.shape[1], table.shape[2]
    early = max(0, reach - first)
    own = count + reach - early
    anywhere = pl.BlockSpec(memory_space=pl.ANY)
    vmem = pl.BlockSpec(memory_space=pltpu.VMEM)
    operands = [samples] + ([rim] if early else []) + [taps, table] + ([] if gate is None else [gate])
    in_specs = [anywhere] + ([anywhere] if early else []) + [vmem, anywhere] + ([] if gate is None else [anywhere])
    out_shape = []
    for widths in sends[: groups // 2]:
        for width in widths:
            out_shape.append(jax.ShapeDtypeStruct((BLOCK, width * columns), jnp.bfloat16))
    for width in sends[-1]:
        out_shape.append(jax.ShapeDtypeStruct((groups // 2, BLOCK, width * columns), jnp.bfloat16))
    scratch = [pltpu.VMEM((2, BLOCK, own * fft_size), jnp.int32)]
    if early:
        scratch.append(pltpu.VMEM((2, BLOCK, early * fft_size), jnp.bfloat16))
    scratch += [
        pltpu.VMEM((groups, depth, columns), jnp.bfloat16),
        pltpu.VMEM((2, count * BLOCK, depth), jnp.bfloat16),
        pltpu.VMEM((groups, BLOCK, count * columns), jnp.bfloat16),
    ]
    if with_rim:
        out_shape.append(jax.ShapeDtypeStruct((2, BLOCK, reach * fft_size), jnp.bfloat16))
        scratch.append(pltpu.VMEM((2, BLOCK, reach * fft_size), jnp.bfloat16))
    scratch += [
        pltpu.SemaphoreType.DMA((2, BLOCK // ROWS)),
        pltpu.SemaphoreType.DMA((groups,)),
        pltpu.SemaphoreType.DMA((groups, max(len(widths) for widths in sends))),
    ]
    geometry = (first, count, sends, with_rim, gate is not None, fft_size, tap_count)
    results = list(
        pl.pallas_call(
            functools.partial(front_kernel, geometry),
            in_specs=in_specs,
            out_specs=[anywhere] * len(out_shape),
            out_shape=out_shape,
            scratch_shapes=scratch,
            compiler_params=pltpu.CompilerParams(vmem_limit_bytes=VMEM_LIMIT),
            cost_estimate=pl.CostEstimate(flops=COST, bytes_accessed=1, transcendentals=0),
        )(*operands)
    )
    pieces = [[results.pop(0) for _ in widths] for widths in sends[: groups // 2]]
    return pieces, results


def gather_kernel(layout, *refs):
    parts, out, held, in_sems, out_sems = refs[:-4], *refs[-4:]
    copies, sends = [], []
    for d, places in enumerate(layout):
        f = 0
        for w, (number, at, start, width) in enumerate(places):
            source = parts[number] if at is None else parts[number].at[at]
            source = source.at[:, start * BLOCK : (start + width) * BLOCK]
            target = held.at[d, :, f * BLOCK : (f + width) * BLOCK]
            copies.append((d, pltpu.make_async_copy(source, target, in_sems.at[d, w])))
            f += width
        sends.append(pltpu.make_async_copy(held.at[d], out.at[d], out_sems.at[d]))
    for _, copy in copies:
        copy.start()
    for d, send in enumerate(sends):
        for owner, copy in copies:
            if owner == d:
                copy.wait()
        send.start()
    for send in sends:
        send.wait()


def gathered(blocks, after):
    operands, layout = [], []
    for block in blocks:
        places = []
        for array, at, start, width in block:
            places.append((len(operands), at, start, width))
            operands.append(array)
        layout.append(tuple(places))
    frames = sum(place[3] for place in layout[0])
    shape = (len(blocks), BLOCK, frames * BLOCK)
    operands += [] if after is None else [after]
    return pl.pallas_call(
        functools.partial(gather_kernel, tuple(layout)),
        in_specs=[pl.BlockSpec(memory_space=pl.ANY)] * len(operands),
        out_specs=pl.BlockSpec(memory_space=pl.ANY),
        out_shape=jax.ShapeDtypeStruct(shape, jnp.bfloat16),
        scratch_shapes=[
            pltpu.VMEM(shape, jnp.bfloat16),
            pltpu.SemaphoreType.DMA((len(blocks), max(len(places) for places in layout))),
            pltpu.SemaphoreType.DMA((len(blocks),)),
        ],
        compiler_params=pltpu.CompilerParams(vmem_limit_bytes=VMEM_LIMIT),
        cost_estimate=pl.CostEstimate(flops=1, bytes_accessed=1, transcendentals=0),
    )(*operands)


def tile_kernel(geometry, first, second, *refs):
    layout, inputs, has_sums, factor = geometry
    count = len(layout)
    arrays = refs[:inputs]
    sums = refs[inputs] if has_sums else None
    refs = refs[inputs + has_sums :]
    out, held, totals = refs[0], refs[1 : 1 + count], refs[1 + count]
    finished = refs[2 + count]
    block_sems, sum_sems, out_sems = refs[-3:]
    slots = totals.shape[0]
    block_copies = []
    for k, places in enumerate(layout):
        for d, (number, at) in enumerate(places):
            source = arrays[number] if at is None else arrays[number].at[at]
            block_copies.append(pltpu.make_async_copy(source, held[k].at[d], block_sems.at[k, d]))
    for copy in block_copies:
        copy.start()

    def copy_in(slot):
        return pltpu.make_async_copy(sums.at[slot], totals.at[slot], sum_sems.at[slot])

    def copy_out(slot):
        return pltpu.make_async_copy(finished.at[slot], out.at[slot], out_sems.at[slot])

    if has_sums:
        for slot in range(slots):
            copy_in(slot).start()
    for copy in block_copies:
        copy.wait()
    if has_sums:
        for slot in range(slots):
            copy_in(slot).wait()

    def correlate(slot, carry):
        a, b = first[slot], second[slot]
        total = None
        for block in held:
            left, right = block[a], block[b]
            turned = []
            for start in range(0, left.shape[1], 2 * LANES):
                turned += [left[:, start + LANES : start + 2 * LANES], -left[:, start : start + LANES]]
            both = jnp.concatenate([left, jnp.concatenate(turned, axis=1)], axis=0)
            term = lax.dot_general(both, right, (((1,), (1,)), ((), ())), preferred_element_type=jnp.float32)
            total = term if total is None else total + term
        if has_sums:
            total = total + totals[slot]
        if factor is not None:
            total = total * factor
        finished[slot] = total.astype(finished.dtype)
        copy_out(slot).start()
        return carry

    lax.fori_loop(0, slots, correlate, 0, unroll=UNROLL)
    for slot in range(slots):
        copy_out(slot).wait()


def tiles(first, second, blocks, sums, factor):
    slots = first.shape[0]
    anywhere = pl.BlockSpec(memory_space=pl.ANY)
    smem = pl.BlockSpec(memory_space=pltpu.SMEM)
    operands, layout = [], []
    for places in blocks:
        if not isinstance(places, list):
            places = [(places, d) for d in range(places.shape[0])]
        numbered = []
        for array, at in places:
            number = next((n for n, known in enumerate(operands) if known is array), len(operands))
            operands += [array] if number == len(operands) else []
            numbered.append((number, at))
        layout.append(tuple(numbered))
    inputs = len(operands)
    operands += [] if sums is None else [sums]
    shape = (slots, 2 * BLOCK, BLOCK)
    kind = jnp.float32 if factor is None else jnp.bfloat16
    scratch = [pltpu.VMEM((len(places),) + operands[places[0][0]].shape[-2:], jnp.bfloat16) for places in layout] + [pltpu.VMEM(shape, jnp.float32), pltpu.VMEM(shape, kind)]
    scratch += [
        pltpu.SemaphoreType.DMA((len(layout), len(layout[0]))),
        pltpu.SemaphoreType.DMA((slots,)),
        pltpu.SemaphoreType.DMA((slots,)),
    ]
    return pl.pallas_call(
        functools.partial(tile_kernel, (tuple(layout), inputs, sums is not None, factor)),
        in_specs=[smem, smem] + [anywhere] * len(operands),
        out_specs=anywhere,
        out_shape=jax.ShapeDtypeStruct(shape, kind),
        scratch_shapes=scratch,
        compiler_params=pltpu.CompilerParams(vmem_limit_bytes=VMEM_LIMIT),
        cost_estimate=pl.CostEstimate(flops=COST, bytes_accessed=1, transcendentals=0),
    )(first, second, *operands)


def dft_table(length):
    index = jnp.arange(length, dtype=jnp.int32)
    phase = index[:, None] * index[None, :] % length
    angle = phase.astype(jnp.float32) * (2.0 * math.pi / length)
    cosine = jnp.cos(angle)
    sine = jnp.sin(angle)
    upper = jnp.stack([cosine, -sine], axis=1)
    lower = jnp.stack([sine, cosine], axis=1)
    return jnp.concatenate([upper, lower], axis=0).astype(jnp.bfloat16)


def tile_products(spectra, slots, tile_count):
    input_count = spectra.shape[0]
    block_count = input_count // BLOCK
    width = spectra.shape[1] * spectra.shape[2] * spectra.shape[3]
    rows_np, cols_np = np.triu_indices(block_count)
    numbers = jnp.arange(tile_count, dtype=jnp.int32)
    match = (slots[:, None] == numbers[None, :]).astype(jnp.int32)
    first = jnp.sum(match * jnp.asarray(rows_np.astype(np.int32))[None, :], axis=1)
    second = jnp.sum(match * jnp.asarray(cols_np.astype(np.int32))[None, :], axis=1)
    swapped = jnp.stack([spectra[:, :, 1], -spectra[:, :, 0]], axis=2)
    plain_blocks = spectra.reshape(block_count, BLOCK, width)
    paired = jnp.stack([plain_blocks, swapped.reshape(block_count, BLOCK, width)], axis=1)
    left_blocks = paired[first]
    right_blocks = plain_blocks[second]
    return jnp.einsum(
        "scuw,svw->scuv", left_blocks, right_blocks, preferred_element_type=jnp.float32
    )


def any_sizes(samples, taps, tile_order):
    inputs_here = samples.shape[1]
    sample_count = samples.shape[2]
    tap_count = taps.shape[0]
    fft_size = taps.shape[1]
    frame_count = sample_count // fft_size
    volts = samples.astype(jnp.bfloat16)
    rim_length = (tap_count - 1) * fft_size
    earlier = passed_along(volts[:, :, sample_count - rim_length :], "pair", 1)
    longer = jnp.concatenate([earlier, volts], axis=2).astype(jnp.float32)
    framed = longer.reshape(2, inputs_here, frame_count + tap_count - 1, fft_size)
    weights = taps.astype(jnp.float32)
    filtered = jnp.zeros((2, inputs_here, frame_count, fft_size), jnp.float32)
    for tap_index in range(tap_count):
        filtered = (
            filtered
            + weights[tap_index][None, None, None, :]
            * framed[:, :, tap_index : tap_index + frame_count, :]
        )
    filtered = filtered.astype(jnp.bfloat16)
    left = jnp.concatenate([filtered[0], filtered[1]], axis=-1)
    table = dft_table(fft_size)
    spectra = jnp.einsum("xfm,mck->xfck", left, table, preferred_element_type=jnp.float32)
    chan_size = lax.axis_size("chan")
    group_width = fft_size // chan_size
    spectra = (
        (spectra * 2.0 ** (-14))
        .astype(jnp.bfloat16)
        .reshape(inputs_here, frame_count, 2, chan_size, group_width)
    )
    turned = lax.all_to_all(spectra, "chan", split_axis=3, concat_axis=0, tiled=True)
    turned = turned.reshape(turned.shape[0], frame_count, 2, group_width)
    tile_count = tile_order.shape[0]
    pair_size = lax.axis_size("pair")
    factor = 1.0 / (frame_count * group_width * pair_size)
    summed = lax.psum_scatter(
        tile_products(turned, tile_order, tile_count), "pair", scatter_dimension=0, tiled=True
    )
    return (summed * factor).astype(jnp.bfloat16)[None]


def per_device(samples, taps, tile_order):
    fft_size = taps.shape[1]
    groups = lax.axis_size("chan")
    pair_size = lax.axis_size("pair")
    me = lax.axis_index("chan").astype(jnp.int32)
    far = groups // 2
    table = jnp.asarray(grouped_table(fft_size, groups))

    slots = tile_order.shape[0] // pair_size
    own_slots = lax.dynamic_slice(tile_order, (lax.axis_index("pair") * slots,), (slots,))
    rows_np, cols_np = np.triu_indices(groups)
    match = (own_slots[:, None] == jnp.arange(tile_order.shape[0], dtype=jnp.int32)[None, :]).astype(jnp.int32)

    def place_of(blocks_np):
        block = jnp.sum(match * jnp.asarray(blocks_np.astype(np.int32))[None, :], axis=1)
        return jnp.where(block // far == me // far, block % far, block ^ me)

    first, second = place_of(rows_np), place_of(cols_np)

    def after(value, *others):
        return lax.optimization_barrier((value, *others))[0]

    def to(mask, value):
        return swapped_with(value, "chan", mask)

    def other_core(value):
        return swapped_with(value, "pair", 1)

    def among_near(value):
        halves = [list(range(start, start + far)) for start in range(0, groups, far)]
        return lax.all_to_all(value, "chan", 0, 0, axis_index_groups=halves, tiled=True)

    apart = range(far, groups)
    FIRST, SECOND, THIRD = PLAN
    end = samples.shape[2] // fft_size
    start_a, start_b = end - FIRST, end - FIRST - SECOND
    made_a, (rim_here,) = front(samples, None, taps, table, None, start_a, FIRST, ((FIRST,),) * far + ((),) * far, True)
    a = {mask: to(mask, made_a[mask - far][0]) for mask in apart}
    rim = passed_along(rim_here, "pair", 1)
    sends = ((SECOND,),) * far + ((SECOND, FIRST),) * far
    made_b, (near_b, near_a) = front(samples, rim, taps, table, made_a[0][0], start_b, SECOND + FIRST, sends, False)
    b = {}
    for mask, gate in zip(apart, [a[far], a[far + 1], a[far + 2], a[far + 3]]):
        b[mask] = to(mask, after(made_b[mask - far][0], gate))
    aa = among_near(near_a)
    bb = among_near(near_b)
    sends = ((THIRD,),) * far + ((THIRD,),) * far
    made_c, (near_c,) = front(samples, rim, taps, table, made_b[0][0], 0, THIRD, sends, False)
    mine = gathered([[(aa, k, 0, FIRST)] for k in range(far)] + [[(a[mask], None, 0, FIRST)] for mask in apart], made_c[0][0])
    other = other_core(mine)
    sums = tiles(first, second, [mine], None, None)
    sums = tiles(first, second, [other], sums, None)
    c = {}
    for mask, gate in zip(apart, [rim, b[far], b[far + 2], b[far + 3]]):
        c[mask] = to(mask, after(made_c[mask - far][0], gate))
    cc = among_near(near_c)
    mine = gathered([[(bb, k, 0, SECOND)] for k in range(far)] + [[(b[mask], None, 0, SECOND)] for mask in apart], sums)
    other = other_core(mine)
    sums = tiles(first, second, [mine], sums, None)
    sums = tiles(first, second, [other], sums, None)
    last = [(cc, k) for k in range(far)] + [(c[mask], None) for mask in apart]
    near_there = other_core(cc)
    there = [(near_there, k) for k in range(far)] + [(other_core(after(c[mask], sums)), None) for mask in apart]
    factor = 1.0 / (end * pair_size * (fft_size // groups))
    sums = tiles(first, second, [last, there], sums, factor)
    return sums.reshape(1, slots, 2, BLOCK, BLOCK)


def chosen(samples, taps, tile_order):
    groups, pair_size = lax.axis_size("chan"), lax.axis_size("pair")
    whole_blocks = samples.shape[1] == BLOCK and taps.shape[1] == groups * LANES
    halves = groups >= 2 and groups & (groups - 1) == 0 and pair_size == 2
    planned = samples.shape[2] == sum(PLAN) * taps.shape[1] and taps.shape[0] - 1 <= PLAN[2]
    if whole_blocks and halves and planned:
        return per_device(samples, taps, tile_order)
    return any_sizes(samples, taps, tile_order)


def solution(mesh):
    in_specs = (P(None, "chan", ("band", "pair")), P(), P())
    out_specs = P(("band", "chan"), "pair", None, None, None)
    return jax.shard_map(chosen, mesh=mesh, in_specs=in_specs, out_specs=out_specs, check_vma=False)
```

```python
import functools
import math

import jax
import jax.numpy as jnp
import ml_dtypes
import numpy as np
from jax import lax
from jax.experimental import pallas as pl
from jax.experimental.pallas import tpu as pltpu
from jax.sharding import PartitionSpec as P

BLOCK = 256
UNROLL = 3
COST = 10**11
LANES = 128
ROWS = 32
SCALE = 2.0**-14
VMEM_LIMIT = 60 * 1024 * 1024

PLAN = (2, 3, 3)


def passed_along(block, axis, distance):
    devices = range(lax.axis_size(axis))
    route = [(i - distance, i) for i in devices if i - distance in devices]
    return lax.ppermute(block, axis, route)


def swapped_with(block, axis, mask):
    return lax.ppermute(block, axis, [(i, i ^ mask) for i in range(lax.axis_size(axis))])


def grouped_table(length, groups):
    index = np.arange(length)
    angle = (index[:, None] * index[None, :] % length).astype(np.float32) * np.float32(2.0 * math.pi / length)
    cosine = np.cos(angle).astype(ml_dtypes.bfloat16).astype(np.float32) * SCALE
    sine = np.sin(angle).astype(ml_dtypes.bfloat16).astype(np.float32) * SCALE
    both = np.stack([cosine, sine], axis=1).reshape(length, 2, groups, length // groups)
    return both.transpose(2, 0, 1, 3).reshape(groups, length, 2 * (length // groups)).astype(ml_dtypes.bfloat16)


def front_kernel(geometry, samples, *refs):
    first, count, sends, with_rim, gated, fft_size, tap_count = geometry
    groups = len(sends)
    reach = tap_count - 1
    early = max(0, reach - first)
    own = count + reach - early
    refs = list(refs)
    rim_in = refs.pop(0) if early else None
    taps, table = refs.pop(0), refs.pop(0)
    if gated:
        refs.pop(0)
    pieces = [[refs.pop(0) for _ in widths] for widths in sends[: groups // 2]]
    near_out = [refs.pop(0) for _ in sends[-1]]
    for j in range(groups // 2, groups):
        pieces.append([out.at[j - groups // 2] for out in near_out])
    rim_out = refs.pop(0) if with_rim else None
    held = refs.pop(0)
    held_rim = refs.pop(0) if early else None
    tables, left, results = refs.pop(0), refs.pop(0), refs.pop(0)
    rim_made = refs.pop(0) if with_rim else None
    in_sems, table_sems, out_sems = refs[:3]
    steps = BLOCK // ROWS
    turns = left.shape[0]
    each, share = steps // turns, BLOCK // turns
    me = lax.axis_index("chan")

    def copies_in(step):
        rows = pl.ds(pl.multiple_of(step * ROWS, ROWS), ROWS)
        lanes = pl.ds((first - reach + early) * fft_size, own * fft_size)
        made = [pltpu.make_async_copy(samples.at[:, rows, lanes], held.at[:, rows, :], in_sems.at[0, step])]
        if early:
            lanes = pl.ds((reach - early) * fft_size, early * fft_size)
            made.append(pltpu.make_async_copy(rim_in.at[:, rows, lanes], held_rim.at[:, rows, :], in_sems.at[1, step]))
        return made

    def copy_table(j):
        group = me ^ (j + groups // 2) if j < groups // 2 else me - lax.rem(me, groups // 2) + (j - groups // 2)
        return pltpu.make_async_copy(table.at[group], tables.at[j], table_sems.at[j])

    def copies_out(j):
        made, f = [], 0
        for w, width in enumerate(sends[j]):
            part = results.at[j, :, f * BLOCK : (f + width) * BLOCK]
            made.append(pltpu.make_async_copy(part, pieces[j][w], out_sems.at[j, w]))
            f += width
        return made

    used = [j for j in range(groups) if sends[j]]
    for step in range(steps):
        for copy in copies_in(step):
            copy.start()
    for j in used:
        copy_table(j).start()

    def filter_rows(turn, step, carry):
        for copy in copies_in(step):
            copy.wait()
        rows = pl.ds(pl.multiple_of(step * ROWS, ROWS), ROWS)
        for part in range(2):
            for start in range(0, fft_size, LANES):
                values = []
                for k in range(early):
                    lanes = slice(k * fft_size + start, k * fft_size + start + LANES)
                    values.append(held_rim[part, rows, lanes].astype(jnp.float32))
                for k in range(own):
                    lanes = slice(k * fft_size + start, k * fft_size + start + LANES)
                    values.append(held[part, rows, lanes].astype(jnp.float32))
                lanes = slice(start, start + LANES)
                weights = [taps[t : t + 1, lanes].astype(jnp.float32) for t in range(tap_count)]
                for f in range(count):
                    total = weights[0] * values[f]
                    for t in range(1, tap_count):
                        total = total + weights[t] * values[f + t]
                    at = pl.ds(pl.multiple_of(f * share + (step - turn * each) * ROWS, ROWS), ROWS)
                    left[turn, part, at, lanes] = total.astype(jnp.bfloat16)
                if with_rim:
                    for t in range(reach):
                        lanes = slice(t * fft_size + start, t * fft_size + start + LANES)
                        rim_made[part, rows, lanes] = values[count + t].astype(jnp.bfloat16)
        return carry


    def transform(j, frames, turn):
        if turn == 0:
            pltpu.make_async_copy(table.at[0], tables.at[j], table_sems.at[j]).wait()

        rows = frames * share
        product = [
            jnp.dot(left[turn, part, :rows, :], tables[j], preferred_element_type=jnp.float32) for part in range(2)
        ]
        real = (product[0][:, :LANES] + product[1][:, LANES:]).astype(jnp.bfloat16)
        imag = (product[1][:, :LANES] - product[0][:, LANES:]).astype(jnp.bfloat16)
        at = slice(turn * share, (turn + 1) * share)
        for f in range(frames):
            results[j, at, f * BLOCK : f * BLOCK + LANES] = real[f * share : (f + 1) * share]
            results[j, at, f * BLOCK + LANES : (f + 1) * BLOCK] = imag[f * share : (f + 1) * share]
        if turn + 1 < turns:
            return
        for k in used:

            @pl.when(j == k)
            def _():
                for copy in copies_out(k):
                    copy.start()

    for turn in range(turns):
        lax.fori_loop(turn * each, (turn + 1) * each, functools.partial(filter_rows, turn), 0)
        if with_rim and turn + 1 == turns:
            rim_copy = pltpu.make_async_copy(rim_made, rim_out, in_sems.at[1, 0])
            rim_copy.start()
        begin = used[0]
        while begin <= used[-1]:
            end = begin
            while end <= used[-1] and sum(sends[end]) == sum(sends[begin]):
                end += 1

            def several(j, carry, frames=sum(sends[begin]), turn=turn):
                transform(j, frames, turn)
                return carry

            lax.fori_loop(begin, end, several, 0, unroll=2)
            begin = end
    if with_rim:
        rim_copy.wait()
    for j in used:
        for copy in copies_out(j):
            copy.wait()


def front(samples, rim, taps, table, gate, first, count, sends, with_rim):
    fft_size = taps.shape[1]
    tap_count = taps.shape[0]
    reach = tap_count - 1
    groups, depth, columns = len(sends), table.shape[1], table.shape[2]
    early = max(0, reach - first)
    own = count + reach - early
    turns = 1
    anywhere = pl.BlockSpec(memory_space=pl.ANY)
    vmem = pl.BlockSpec(memory_space=pltpu.VMEM)
    operands = [samples] + ([rim] if early else []) + [taps, table] + ([] if gate is None else [gate])
    in_specs = [anywhere] + ([anywhere] if early else []) + [vmem, anywhere] + ([] if gate is None else [anywhere])
    out_shape = []
    for widths in sends[: groups // 2]:
        for width in widths:
            out_shape.append(jax.ShapeDtypeStruct((BLOCK, width * columns), jnp.bfloat16))
    for width in sends[-1]:
        out_shape.append(jax.ShapeDtypeStruct((groups // 2, BLOCK, width * columns), jnp.bfloat16))
    scratch = [pltpu.VMEM((2, BLOCK, own * fft_size), jnp.int32)]
    if early:
        scratch.append(pltpu.VMEM((2, BLOCK, early * fft_size), jnp.bfloat16))
    scratch += [
        pltpu.VMEM((groups, depth, columns), jnp.bfloat16),
        pltpu.VMEM((turns, 2, count * BLOCK // turns, depth), jnp.bfloat16),
        pltpu.VMEM((groups, BLOCK, count * columns), jnp.bfloat16),
    ]
    if with_rim:
        out_shape.append(jax.ShapeDtypeStruct((2, BLOCK, reach * fft_size), jnp.bfloat16))
        scratch.append(pltpu.VMEM((2, BLOCK, reach * fft_size), jnp.bfloat16))
    scratch += [
        pltpu.SemaphoreType.DMA((2, BLOCK // ROWS)),
        pltpu.SemaphoreType.DMA((groups,)),
        pltpu.SemaphoreType.DMA((groups, max(len(widths) for widths in sends))),
    ]
    geometry = (first, count, sends, with_rim, gate is not None, fft_size, tap_count)
    results = list(
        pl.pallas_call(
            functools.partial(front_kernel, geometry),
            in_specs=in_specs,
            out_specs=[anywhere] * len(out_shape),
            out_shape=out_shape,
            scratch_shapes=scratch,
            compiler_params=pltpu.CompilerParams(vmem_limit_bytes=VMEM_LIMIT),
            cost_estimate=pl.CostEstimate(flops=COST, bytes_accessed=1, transcendentals=0),
        )(*operands)
    )
    pieces = [[results.pop(0) for _ in widths] for widths in sends[: groups // 2]]
    return pieces, results


def gather_kernel(layout, *refs):
    parts, out, held, in_sems, out_sems = refs[:-4], *refs[-4:]
    copies, sends = [], []
    for d, places in enumerate(layout):
        f = 0
        for w, (number, at, start, width) in enumerate(places):
            source = parts[number] if at is None else parts[number].at[at]
            source = source.at[:, start * BLOCK : (start + width) * BLOCK]
            target = held.at[d, :, f * BLOCK : (f + width) * BLOCK]
            copies.append((d, pltpu.make_async_copy(source, target, in_sems.at[d, w])))
            f += width
        sends.append(pltpu.make_async_copy(held.at[d], out.at[d], out_sems.at[d]))
    for _, copy in copies:
        copy.start()
    for d, send in enumerate(sends):
        for owner, copy in copies:
            if owner == d:
                copy.wait()
        send.start()
    for send in sends:
        send.wait()


def gathered(blocks, after):
    operands, layout = [], []
    for block in blocks:
        places = []
        for array, at, start, width in block:
            places.append((len(operands), at, start, width))
            operands.append(array)
        layout.append(tuple(places))
    frames = sum(place[3] for place in layout[0])
    shape = (len(blocks), BLOCK, frames * BLOCK)
    operands += [] if after is None else [after]
    return pl.pallas_call(
        functools.partial(gather_kernel, tuple(layout)),
        in_specs=[pl.BlockSpec(memory_space=pl.ANY)] * len(operands),
        out_specs=pl.BlockSpec(memory_space=pl.ANY),
        out_shape=jax.ShapeDtypeStruct(shape, jnp.bfloat16),
        scratch_shapes=[
            pltpu.VMEM(shape, jnp.bfloat16),
            pltpu.SemaphoreType.DMA((len(blocks), max(len(places) for places in layout))),
            pltpu.SemaphoreType.DMA((len(blocks),)),
        ],
        compiler_params=pltpu.CompilerParams(vmem_limit_bytes=VMEM_LIMIT),
        cost_estimate=pl.CostEstimate(flops=1, bytes_accessed=1, transcendentals=0),
    )(*operands)


def tile_kernel(geometry, first, second, *refs):
    layout, inputs, has_sums, factor = geometry
    count = len(layout)
    arrays = refs[:inputs]
    sums = refs[inputs] if has_sums else None
    refs = refs[inputs + has_sums :]
    out, held, totals = refs[0], refs[1 : 1 + count], refs[1 + count]
    finished = refs[2 + count]
    partial = refs[3 + count] if count == 2 else None
    block_sems, sum_sems, out_sems = refs[-3:]
    slots = totals.shape[0]
    copies = []
    for k, places in enumerate(layout):
        copies.append([])
        for d, (number, at) in enumerate(places):
            source = arrays[number] if at is None else arrays[number].at[at]
            copies[k].append(pltpu.make_async_copy(source, held[k].at[d], block_sems.at[k, d]))
    for copy in copies[0]:
        copy.start()

    def copy_in(slot):
        return pltpu.make_async_copy(sums.at[slot], totals.at[slot], sum_sems.at[slot])

    def copy_out(slot):
        return pltpu.make_async_copy(finished.at[slot], out.at[slot], out_sems.at[slot])

    stage = -(-slots // 3)
    stages = [range(start, min(start + stage, slots)) for start in range(0, slots, stage)]
    if has_sums and count == 1:
        for slot in stages[0]:
            copy_in(slot).start()
    for copy in copies[0]:
        copy.wait()

    def term_of(block, slot):
        left, right = block[first[slot]], block[second[slot]]
        turned = []
        for start in range(0, left.shape[1], 2 * LANES):
            turned += [left[:, start + LANES : start + 2 * LANES], -left[:, start : start + LANES]]
        both = jnp.concatenate([left, jnp.concatenate(turned, axis=1)], axis=0)
        return lax.dot_general(both, right, (((1,), (1,)), ((), ())), preferred_element_type=jnp.float32)

    def begin(slot, carry):
        partial[slot] = term_of(held[0], slot)
        return carry

    if count == 2:
        for copy in copies[1]:
            copy.start()
        for slot in range(slots):
            copy_in(slot).start()
        lax.fori_loop(0, slots, begin, 0, unroll=6)
        for copy in copies[1]:
            copy.wait()

    def correlate(slot, carry):
        total = term_of(held[-1], slot)
        if count == 2:
            total = total + partial[slot]
        if has_sums:
            total = total + totals[slot]
        if factor is not None:
            total = total * factor
        finished[slot] = total.astype(finished.dtype)
        copy_out(slot).start()
        return carry

    for number, several in enumerate(stages):
        if has_sums:
            for slot in several:
                copy_in(slot).wait()
            for slot in stages[number + 1] if number + 1 < len(stages) and count == 1 else ():
                copy_in(slot).start()
        lax.fori_loop(several.start, several.stop, correlate, 0, unroll=UNROLL if factor is None else 6)
    for slot in range(slots):
        copy_out(slot).wait()


def tiles(first, second, blocks, sums, factor):
    slots = first.shape[0]
    anywhere = pl.BlockSpec(memory_space=pl.ANY)
    smem = pl.BlockSpec(memory_space=pltpu.SMEM)
    operands, layout = [], []
    for places in blocks:
        if not isinstance(places, list):
            places = [(places, d) for d in range(places.shape[0])]
        numbered = []
        for array, at in places:
            number = next((n for n, known in enumerate(operands) if known is array), len(operands))
            operands += [array] if number == len(operands) else []
            numbered.append((number, at))
        layout.append(tuple(numbered))
    inputs = len(operands)
    operands += [] if sums is None else [sums]
    shape = (slots, 2 * BLOCK, BLOCK)
    kind = jnp.float32 if factor is None else jnp.bfloat16
    scratch = [pltpu.VMEM((len(places),) + operands[places[0][0]].shape[-2:], jnp.bfloat16) for places in layout] + [pltpu.VMEM(shape, jnp.float32), pltpu.VMEM(shape, kind)]
    scratch += [pltpu.VMEM(shape, jnp.float32)] if len(blocks) == 2 else []
    scratch += [
        pltpu.SemaphoreType.DMA((len(layout), len(layout[0]))),
        pltpu.SemaphoreType.DMA((slots,)),
        pltpu.SemaphoreType.DMA((slots,)),
    ]
    return pl.pallas_call(
        functools.partial(tile_kernel, (tuple(layout), inputs, sums is not None, factor)),
        in_specs=[smem, smem] + [anywhere] * len(operands),
        out_specs=anywhere,
        out_shape=jax.ShapeDtypeStruct(shape, kind),
        scratch_shapes=scratch,
        compiler_params=pltpu.CompilerParams(vmem_limit_bytes=VMEM_LIMIT),
        cost_estimate=pl.CostEstimate(flops=COST, bytes_accessed=1, transcendentals=0),
    )(first, second, *operands)


def dft_table(length):
    index = jnp.arange(length, dtype=jnp.int32)
    phase = index[:, None] * index[None, :] % length
    angle = phase.astype(jnp.float32) * (2.0 * math.pi / length)
    cosine = jnp.cos(angle)
    sine = jnp.sin(angle)
    upper = jnp.stack([cosine, -sine], axis=1)
    lower = jnp.stack([sine, cosine], axis=1)
    return jnp.concatenate([upper, lower], axis=0).astype(jnp.bfloat16)


def tile_products(spectra, slots, tile_count):
    input_count = spectra.shape[0]
    block_count = input_count // BLOCK
    width = spectra.shape[1] * spectra.shape[2] * spectra.shape[3]
    rows_np, cols_np = np.triu_indices(block_count)
    numbers = jnp.arange(tile_count, dtype=jnp.int32)
    match = (slots[:, None] == numbers[None, :]).astype(jnp.int32)
    first = jnp.sum(match * jnp.asarray(rows_np.astype(np.int32))[None, :], axis=1)
    second = jnp.sum(match * jnp.asarray(cols_np.astype(np.int32))[None, :], axis=1)
    swapped = jnp.stack([spectra[:, :, 1], -spectra[:, :, 0]], axis=2)
    plain_blocks = spectra.reshape(block_count, BLOCK, width)
    paired = jnp.stack([plain_blocks, swapped.reshape(block_count, BLOCK, width)], axis=1)
    left_blocks = paired[first]
    right_blocks = plain_blocks[second]
    return jnp.einsum(
        "scuw,svw->scuv", left_blocks, right_blocks, preferred_element_type=jnp.float32
    )


def any_sizes(samples, taps, tile_order):
    inputs_here = samples.shape[1]
    sample_count = samples.shape[2]
    tap_count = taps.shape[0]
    fft_size = taps.shape[1]
    frame_count = sample_count // fft_size
    volts = samples.astype(jnp.bfloat16)
    rim_length = (tap_count - 1) * fft_size
    earlier = passed_along(volts[:, :, sample_count - rim_length :], "pair", 1)
    longer = jnp.concatenate([earlier, volts], axis=2).astype(jnp.float32)
    framed = longer.reshape(2, inputs_here, frame_count + tap_count - 1, fft_size)
    weights = taps.astype(jnp.float32)
    filtered = jnp.zeros((2, inputs_here, frame_count, fft_size), jnp.float32)
    for tap_index in range(tap_count):
        filtered = (
            filtered
            + weights[tap_index][None, None, None, :]
            * framed[:, :, tap_index : tap_index + frame_count, :]
        )
    filtered = filtered.astype(jnp.bfloat16)
    left = jnp.concatenate([filtered[0], filtered[1]], axis=-1)
    table = dft_table(fft_size)
    spectra = jnp.einsum("xfm,mck->xfck", left, table, preferred_element_type=jnp.float32)
    chan_size = lax.axis_size("chan")
    group_width = fft_size // chan_size
    spectra = (
        (spectra * 2.0 ** (-14))
        .astype(jnp.bfloat16)
        .reshape(inputs_here, frame_count, 2, chan_size, group_width)
    )
    turned = lax.all_to_all(spectra, "chan", split_axis=3, concat_axis=0, tiled=True)
    turned = turned.reshape(turned.shape[0], frame_count, 2, group_width)
    tile_count = tile_order.shape[0]
    pair_size = lax.axis_size("pair")
    factor = 1.0 / (frame_count * group_width * pair_size)
    summed = lax.psum_scatter(
        tile_products(turned, tile_order, tile_count), "pair", scatter_dimension=0, tiled=True
    )
    return (summed * factor).astype(jnp.bfloat16)[None]


def per_device(samples, taps, tile_order):
    fft_size = taps.shape[1]
    groups = lax.axis_size("chan")
    pair_size = lax.axis_size("pair")
    me = lax.axis_index("chan").astype(jnp.int32)
    far = groups // 2
    table = jnp.asarray(grouped_table(fft_size, groups))

    slots = tile_order.shape[0] // pair_size
    own_slots = lax.dynamic_slice(tile_order, (lax.axis_index("pair") * slots,), (slots,))
    rows_np, cols_np = np.triu_indices(groups)
    match = (own_slots[:, None] == jnp.arange(tile_order.shape[0], dtype=jnp.int32)[None, :]).astype(jnp.int32)

    def place_of(blocks_np):
        block = jnp.sum(match * jnp.asarray(blocks_np.astype(np.int32))[None, :], axis=1)
        return jnp.where(block // far == me // far, block % far, block ^ me)

    first, second = place_of(rows_np), place_of(cols_np)

    def after(value, *others):
        return lax.optimization_barrier((value, *others))[0]

    def to(mask, value):
        return swapped_with(value, "chan", mask)

    def other_core(value):
        return swapped_with(value, "pair", 1)

    def among_near(value):
        halves = [list(range(start, start + far)) for start in range(0, groups, far)]
        return lax.all_to_all(value, "chan", 0, 0, axis_index_groups=halves, tiled=True)

    apart = range(far, groups)
    FIRST, SECOND, THIRD = PLAN
    end = samples.shape[2] // fft_size
    start_a, start_b = end - FIRST, end - FIRST - SECOND
    made_a, (rim_here,) = front(samples, None, taps, table, None, start_a, FIRST, ((FIRST,),) * far + ((),) * far, True)
    a = {mask: to(mask, made_a[mask - far][0]) for mask in apart}
    rim = passed_along(rim_here, "pair", 1)
    sends = ((SECOND,),) * far + ((),) * far
    made_b, _ = front(samples, rim, taps, table, made_a[0][0], start_b, SECOND, sends, False)
    sends = ((),) * far + ((SECOND, FIRST),) * far
    _, (near_b, near_a) = front(samples, rim, taps, table, made_b[0][0], start_b, SECOND + FIRST, sends, False)
    b = {}
    for mask, gate in zip(apart, [a[far], a[far + 1], a[far + 2], a[far + 3]]):
        b[mask] = to(mask, after(made_b[mask - far][0], gate))
    aa = among_near(near_a)
    bb = among_near(near_b)
    sends = ((THIRD,),) * far + ((THIRD,),) * far
    made_c, (near_c,) = front(samples, rim, taps, table, near_b, 0, THIRD, sends, False)
    mine = gathered([[(aa, k, 0, FIRST)] for k in range(far)] + [[(a[mask], None, 0, FIRST)] for mask in apart], made_c[0][0])
    other = other_core(mine)
    sums = tiles(first, second, [mine], None, None)
    sums = tiles(first, second, [other], sums, None)
    c = {}
    for mask, gate in zip(apart, [rim, b[far], b[far + 2], b[far + 3]]):
        c[mask] = to(mask, after(made_c[mask - far][0], gate))
    cc = among_near(near_c)
    mine = gathered([[(bb, k, 0, SECOND)] for k in range(far)] + [[(b[mask], None, 0, SECOND)] for mask in apart], sums)
    other = other_core(mine)
    sums = tiles(first, second, [mine], sums, None)
    sums = tiles(first, second, [other], sums, None)
    last = [(cc, k) for k in range(far)] + [(c[mask], None) for mask in apart]
    near_there = other_core(cc)
    there = [(near_there, k) for k in range(far)] + [(other_core(after(c[mask], sums)), None) for mask in apart]
    factor = 1.0 / (end * pair_size * (fft_size // groups))
    sums = tiles(first, second, [last, there], sums, factor)
    return sums.reshape(1, slots, 2, BLOCK, BLOCK)


def chosen(samples, taps, tile_order):
    groups, pair_size = lax.axis_size("chan"), lax.axis_size("pair")
    whole_blocks = samples.shape[1] == BLOCK and taps.shape[1] == groups * LANES
    halves = groups >= 2 and groups & (groups - 1) == 0 and pair_size == 2
    planned = samples.shape[2] == sum(PLAN) * taps.shape[1] and taps.shape[0] - 1 <= PLAN[2]
    if whole_blocks and halves and planned:
        return per_device(samples, taps, tile_order)
    return any_sizes(samples, taps, tile_order)


def solution(mesh):
    in_specs = (P(None, "chan", ("band", "pair")), P(), P())
    out_specs = P(("band", "chan"), "pair", None, None, None)
    return jax.shard_map(chosen, mesh=mesh, in_specs=in_specs, out_specs=out_specs, check_vma=False)
```

```python
import functools
import math

import jax
import jax.numpy as jnp
import ml_dtypes
import numpy as np
from jax import lax
from jax.experimental import pallas as pl
from jax.experimental.pallas import tpu as pltpu
from jax.sharding import PartitionSpec as P

BLOCK = 256
UNROLL = 3
COST = 10**11
LANES = 128
ROWS = 32
SCALE = 2.0**-14
VMEM_LIMIT = 63 * 1024 * 1024

PLAN = (1, 3, 4)


def passed_along(block, axis, distance):
    devices = range(lax.axis_size(axis))
    route = [(i - distance, i) for i in devices if i - distance in devices]
    return lax.ppermute(block, axis, route)


def swapped_with(block, axis, mask):
    return lax.ppermute(block, axis, [(i, i ^ mask) for i in range(lax.axis_size(axis))])


def grouped_table(length, groups):
    index = np.arange(length)
    angle = (index[:, None] * index[None, :] % length).astype(np.float32) * np.float32(2.0 * math.pi / length)
    cosine = np.cos(angle).astype(ml_dtypes.bfloat16).astype(np.float32) * SCALE
    sine = np.sin(angle).astype(ml_dtypes.bfloat16).astype(np.float32) * SCALE
    both = np.stack([cosine, sine], axis=1).reshape(length, 2, groups, length // groups)
    return both.transpose(2, 0, 1, 3).reshape(groups, length, 2 * (length // groups)).astype(ml_dtypes.bfloat16)


def front_kernel(geometry, samples, *refs):
    first, count, sends, with_rim, gated, fft_size, tap_count = geometry
    groups = len(sends)
    reach = tap_count - 1
    early = max(0, reach - first)
    own = count + reach - early
    refs = list(refs)
    rim_in = refs.pop(0) if early else None
    taps, table = refs.pop(0), refs.pop(0)
    if gated:
        refs.pop(0)
    pieces = [[refs.pop(0) for _ in widths] for widths in sends[: groups // 2]]
    near_out = [refs.pop(0) for _ in sends[-1]]
    for j in range(groups // 2, groups):
        pieces.append([out.at[j - groups // 2] for out in near_out])
    rim_out = refs.pop(0) if with_rim else None
    held = refs.pop(0)
    held_rim = refs.pop(0) if early else None
    tables, left, results = refs.pop(0), refs.pop(0), refs.pop(0)
    rim_made = refs.pop(0) if with_rim else None
    in_sems, table_sems, out_sems = refs[:3]
    steps = BLOCK // ROWS
    turns = left.shape[0]
    each, share = steps // turns, BLOCK // turns
    me = lax.axis_index("chan")

    def copies_in(step):
        rows = pl.ds(pl.multiple_of(step * ROWS, ROWS), ROWS)
        lanes = pl.ds((first - reach + early) * fft_size, own * fft_size)
        made = [pltpu.make_async_copy(samples.at[:, rows, lanes], held.at[:, rows, :], in_sems.at[0, step])]
        if early:
            lanes = pl.ds((reach - early) * fft_size, early * fft_size)
            made.append(pltpu.make_async_copy(rim_in.at[:, rows, lanes], held_rim.at[:, rows, :], in_sems.at[1, step]))
        return made

    def copy_table(j):
        group = me ^ (j + groups // 2) if j < groups // 2 else me - lax.rem(me, groups // 2) + (j - groups // 2)
        return pltpu.make_async_copy(table.at[group], tables.at[j], table_sems.at[j])

    def copies_out(j):
        made, f = [], 0
        for w, width in enumerate(sends[j]):
            part = results.at[j, :, f * BLOCK : (f + width) * BLOCK]
            made.append(pltpu.make_async_copy(part, pieces[j][w], out_sems.at[j, w]))
            f += width
        return made

    used = [j for j in range(groups) if sends[j]]
    for step in range(steps):
        for copy in copies_in(step):
            copy.start()
    for j in used:
        copy_table(j).start()

    def filter_rows(turn, step, carry):
        for copy in copies_in(step):
            copy.wait()
        rows = pl.ds(pl.multiple_of(step * ROWS, ROWS), ROWS)
        for part in range(2):
            for start in range(0, fft_size, LANES):
                values = []
                for k in range(early):
                    lanes = slice(k * fft_size + start, k * fft_size + start + LANES)
                    values.append(held_rim[part, rows, lanes].astype(jnp.float32))
                for k in range(own):
                    lanes = slice(k * fft_size + start, k * fft_size + start + LANES)
                    values.append(held[part, rows, lanes].astype(jnp.float32))
                lanes = slice(start, start + LANES)
                weights = [taps[t : t + 1, lanes].astype(jnp.float32) for t in range(tap_count)]
                for f in range(count):
                    total = weights[0] * values[f]
                    for t in range(1, tap_count):
                        total = total + weights[t] * values[f + t]
                    at = pl.ds(pl.multiple_of(f * share + (step - turn * each) * ROWS, ROWS), ROWS)
                    left[turn, part, at, lanes] = total.astype(jnp.bfloat16)
                if with_rim:
                    for t in range(reach):
                        lanes = slice(t * fft_size + start, t * fft_size + start + LANES)
                        rim_made[part, rows, lanes] = values[count + t].astype(jnp.bfloat16)
        return carry


    def transform(j, frames, turn):
        if turn == 0:
            pltpu.make_async_copy(table.at[0], tables.at[j], table_sems.at[j]).wait()

        rows = frames * share
        product = [
            jnp.dot(left[turn, part, :rows, :], tables[j], preferred_element_type=jnp.float32) for part in range(2)
        ]
        real = (product[0][:, :LANES] + product[1][:, LANES:]).astype(jnp.bfloat16)
        imag = (product[1][:, :LANES] - product[0][:, LANES:]).astype(jnp.bfloat16)
        at = slice(turn * share, (turn + 1) * share)
        for f in range(frames):
            results[j, at, f * BLOCK : f * BLOCK + LANES] = real[f * share : (f + 1) * share]
            results[j, at, f * BLOCK + LANES : (f + 1) * BLOCK] = imag[f * share : (f + 1) * share]
        if turn + 1 < turns:
            return
        for k in used:

            @pl.when(j == k)
            def _():
                for copy in copies_out(k):
                    copy.start()

    for turn in range(turns):
        lax.fori_loop(turn * each, (turn + 1) * each, functools.partial(filter_rows, turn), 0)
        if with_rim and turn + 1 == turns:
            rim_copy = pltpu.make_async_copy(rim_made, rim_out, in_sems.at[1, 0])
            rim_copy.start()
        begin = used[0]
        while begin <= used[-1]:
            end = begin
            while end <= used[-1] and sum(sends[end]) == sum(sends[begin]):
                end += 1

            def several(j, carry, frames=sum(sends[begin]), turn=turn):
                transform(j, frames, turn)
                return carry

            lax.fori_loop(begin, end, several, 0, unroll=2)
            begin = end
    if with_rim:
        rim_copy.wait()
    for j in used:
        for copy in copies_out(j):
            copy.wait()


def front(samples, rim, taps, table, gate, first, count, sends, with_rim):
    fft_size = taps.shape[1]
    tap_count = taps.shape[0]
    reach = tap_count - 1
    groups, depth, columns = len(sends), table.shape[1], table.shape[2]
    early = max(0, reach - first)
    own = count + reach - early
    turns = 1
    anywhere = pl.BlockSpec(memory_space=pl.ANY)
    vmem = pl.BlockSpec(memory_space=pltpu.VMEM)
    operands = [samples] + ([rim] if early else []) + [taps, table] + ([] if gate is None else [gate])
    in_specs = [anywhere] + ([anywhere] if early else []) + [vmem, anywhere] + ([] if gate is None else [anywhere])
    out_shape = []
    for widths in sends[: groups // 2]:
        for width in widths:
            out_shape.append(jax.ShapeDtypeStruct((BLOCK, width * columns), jnp.bfloat16))
    for width in sends[-1]:
        out_shape.append(jax.ShapeDtypeStruct((groups // 2, BLOCK, width * columns), jnp.bfloat16))
    scratch = [pltpu.VMEM((2, BLOCK, own * fft_size), jnp.int32)]
    if early:
        scratch.append(pltpu.VMEM((2, BLOCK, early * fft_size), jnp.bfloat16))
    scratch += [
        pltpu.VMEM((groups, depth, columns), jnp.bfloat16),
        pltpu.VMEM((turns, 2, count * BLOCK // turns, depth), jnp.bfloat16),
        pltpu.VMEM((groups, BLOCK, count * columns), jnp.bfloat16),
    ]
    if with_rim:
        out_shape.append(jax.ShapeDtypeStruct((2, BLOCK, reach * fft_size), jnp.bfloat16))
        scratch.append(pltpu.VMEM((2, BLOCK, reach * fft_size), jnp.bfloat16))
    scratch += [
        pltpu.SemaphoreType.DMA((2, BLOCK // ROWS)),
        pltpu.SemaphoreType.DMA((groups,)),
        pltpu.SemaphoreType.DMA((groups, max(len(widths) for widths in sends))),
    ]
    geometry = (first, count, sends, with_rim, gate is not None, fft_size, tap_count)
    results = list(
        pl.pallas_call(
            functools.partial(front_kernel, geometry),
            in_specs=in_specs,
            out_specs=[anywhere] * len(out_shape),
            out_shape=out_shape,
            scratch_shapes=scratch,
            compiler_params=pltpu.CompilerParams(vmem_limit_bytes=VMEM_LIMIT),
            cost_estimate=pl.CostEstimate(flops=COST, bytes_accessed=1, transcendentals=0),
        )(*operands)
    )
    pieces = [[results.pop(0) for _ in widths] for widths in sends[: groups // 2]]
    return pieces, results


def gather_kernel(layout, *refs):
    parts, out, held, in_sems, out_sems = refs[:-4], *refs[-4:]
    copies, sends = [], []
    for d, places in enumerate(layout):
        f = 0
        for w, (number, at, start, width) in enumerate(places):
            source = parts[number] if at is None else parts[number].at[at]
            source = source.at[:, start * BLOCK : (start + width) * BLOCK]
            target = held.at[d, :, f * BLOCK : (f + width) * BLOCK]
            copies.append((d, pltpu.make_async_copy(source, target, in_sems.at[d, w])))
            f += width
        sends.append(pltpu.make_async_copy(held.at[d], out.at[d], out_sems.at[d]))
    for _, copy in copies:
        copy.start()
    for d, send in enumerate(sends):
        for owner, copy in copies:
            if owner == d:
                copy.wait()
        send.start()
    for send in sends:
        send.wait()


def gathered(blocks, after):
    operands, layout = [], []
    for block in blocks:
        places = []
        for array, at, start, width in block:
            places.append((len(operands), at, start, width))
            operands.append(array)
        layout.append(tuple(places))
    frames = sum(place[3] for place in layout[0])
    shape = (len(blocks), BLOCK, frames * BLOCK)
    operands += [] if after is None else [after]
    return pl.pallas_call(
        functools.partial(gather_kernel, tuple(layout)),
        in_specs=[pl.BlockSpec(memory_space=pl.ANY)] * len(operands),
        out_specs=pl.BlockSpec(memory_space=pl.ANY),
        out_shape=jax.ShapeDtypeStruct(shape, jnp.bfloat16),
        scratch_shapes=[
            pltpu.VMEM(shape, jnp.bfloat16),
            pltpu.SemaphoreType.DMA((len(blocks), max(len(places) for places in layout))),
            pltpu.SemaphoreType.DMA((len(blocks),)),
        ],
        compiler_params=pltpu.CompilerParams(vmem_limit_bytes=VMEM_LIMIT),
        cost_estimate=pl.CostEstimate(flops=1, bytes_accessed=1, transcendentals=0),
    )(*operands)


def tile_kernel(geometry, first, second, *refs):
    layout, inputs, has_sums, factor = geometry
    count = len(layout)
    arrays = refs[:inputs]
    sums = refs[inputs] if has_sums else None
    refs = refs[inputs + has_sums :]
    out, held, totals = refs[0], refs[1 : 1 + count], refs[1 + count]
    finished = refs[2 + count]
    partial = refs[3 + count] if count == 2 else None
    block_sems, sum_sems, out_sems = refs[-3:]
    slots = totals.shape[0]
    copies = []
    for k, places in enumerate(layout):
        copies.append([])
        for d, (number, at) in enumerate(places):
            source = arrays[number] if at is None else arrays[number].at[at]
            copies[k].append(pltpu.make_async_copy(source, held[k].at[d], block_sems.at[k, d]))
    for copy in copies[0]:
        copy.start()

    def copy_in(slot):
        return pltpu.make_async_copy(sums.at[slot], totals.at[slot], sum_sems.at[slot])

    def copy_out(slot):
        return pltpu.make_async_copy(finished.at[slot], out.at[slot], out_sems.at[slot])

    stage = -(-slots // 3)
    stages = [range(start, min(start + stage, slots)) for start in range(0, slots, stage)]
    if has_sums and count == 1:
        for slot in stages[0]:
            copy_in(slot).start()
    for copy in copies[0]:
        copy.wait()

    def term_of(block, slot):
        left, right = block[first[slot]], block[second[slot]]
        turned = []
        for start in range(0, left.shape[1], 2 * LANES):
            turned += [left[:, start + LANES : start + 2 * LANES], -left[:, start : start + LANES]]
        both = jnp.concatenate([left, jnp.concatenate(turned, axis=1)], axis=0)
        return lax.dot_general(both, right, (((1,), (1,)), ((), ())), preferred_element_type=jnp.float32)

    def begin(slot, carry):
        partial[slot] = term_of(held[0], slot)
        return carry

    if count == 2:
        for copy in copies[1]:
            copy.start()
        for slot in range(slots):
            copy_in(slot).start()
        lax.fori_loop(0, slots, begin, 0, unroll=6)
        for copy in copies[1]:
            copy.wait()

    def correlate(slot, carry):
        total = term_of(held[-1], slot)
        if count == 2:
            total = total + partial[slot]
        if has_sums:
            total = total + totals[slot]
        if factor is not None:
            total = total * factor
        finished[slot] = total.astype(finished.dtype)
        copy_out(slot).start()
        return carry

    for number, several in enumerate(stages):
        if has_sums:
            for slot in several:
                copy_in(slot).wait()
            for slot in stages[number + 1] if number + 1 < len(stages) and count == 1 else ():
                copy_in(slot).start()
        lax.fori_loop(several.start, several.stop, correlate, 0, unroll=UNROLL if factor is None else 6)
    for slot in range(slots):
        copy_out(slot).wait()


def tiles(first, second, blocks, sums, factor):
    slots = first.shape[0]
    anywhere = pl.BlockSpec(memory_space=pl.ANY)
    smem = pl.BlockSpec(memory_space=pltpu.SMEM)
    operands, layout = [], []
    for places in blocks:
        if not isinstance(places, list):
            places = [(places, d) for d in range(places.shape[0])]
        numbered = []
        for array, at in places:
            number = next((n for n, known in enumerate(operands) if known is array), len(operands))
            operands += [array] if number == len(operands) else []
            numbered.append((number, at))
        layout.append(tuple(numbered))
    inputs = len(operands)
    operands += [] if sums is None else [sums]
    shape = (slots, 2 * BLOCK, BLOCK)
    kind = jnp.float32 if factor is None else jnp.bfloat16
    scratch = [pltpu.VMEM((len(places),) + operands[places[0][0]].shape[-2:], jnp.bfloat16) for places in layout] + [pltpu.VMEM(shape, jnp.float32), pltpu.VMEM(shape, kind)]
    scratch += [pltpu.VMEM(shape, jnp.float32)] if len(blocks) == 2 else []
    scratch += [
        pltpu.SemaphoreType.DMA((len(layout), len(layout[0]))),
        pltpu.SemaphoreType.DMA((slots,)),
        pltpu.SemaphoreType.DMA((slots,)),
    ]
    return pl.pallas_call(
        functools.partial(tile_kernel, (tuple(layout), inputs, sums is not None, factor)),
        in_specs=[smem, smem] + [anywhere] * len(operands),
        out_specs=anywhere,
        out_shape=jax.ShapeDtypeStruct(shape, kind),
        scratch_shapes=scratch,
        compiler_params=pltpu.CompilerParams(vmem_limit_bytes=VMEM_LIMIT),
        cost_estimate=pl.CostEstimate(flops=COST, bytes_accessed=1, transcendentals=0),
    )(first, second, *operands)


def slots_kernel(groups, tile_order, gate, first, second):
    me, core = lax.axis_index("chan"), lax.axis_index("pair")
    slots, far = first.shape[0], groups // 2
    starts = [a * groups - a * (a - 1) // 2 for a in range(groups)]
    my_half = me >= far

    def place(block):
        return jnp.where((block >= far) == my_half, lax.rem(block, far), block ^ me)

    def one(slot, carry):
        tile = tile_order[core * slots + slot]
        row, begin = jnp.int32(0), jnp.int32(0)
        for a in range(1, groups):
            row = row + jnp.where(tile >= starts[a], 1, 0)
            begin = jnp.where(tile >= starts[a], starts[a], begin)
        first[slot] = place(row)
        second[slot] = place(tile - begin + row)
        return carry

    lax.fori_loop(0, slots, one, 0)


def slot_places(tile_order, groups, slots, gate):
    smem = pl.BlockSpec(memory_space=pltpu.SMEM)
    places = jax.ShapeDtypeStruct((slots,), jnp.int32)
    return pl.pallas_call(
        functools.partial(slots_kernel, groups),
        in_specs=[smem, pl.BlockSpec(memory_space=pl.ANY)],
        out_specs=[smem, smem],
        out_shape=[places, places],
        cost_estimate=pl.CostEstimate(flops=COST, bytes_accessed=1, transcendentals=0),
    )(tile_order, gate)


def dft_table(length):
    index = jnp.arange(length, dtype=jnp.int32)
    phase = index[:, None] * index[None, :] % length
    angle = phase.astype(jnp.float32) * (2.0 * math.pi / length)
    cosine = jnp.cos(angle)
    sine = jnp.sin(angle)
    upper = jnp.stack([cosine, -sine], axis=1)
    lower = jnp.stack([sine, cosine], axis=1)
    return jnp.concatenate([upper, lower], axis=0).astype(jnp.bfloat16)


def tile_products(spectra, slots, tile_count):
    input_count = spectra.shape[0]
    block_count = input_count // BLOCK
    width = spectra.shape[1] * spectra.shape[2] * spectra.shape[3]
    rows_np, cols_np = np.triu_indices(block_count)
    numbers = jnp.arange(tile_count, dtype=jnp.int32)
    match = (slots[:, None] == numbers[None, :]).astype(jnp.int32)
    first = jnp.sum(match * jnp.asarray(rows_np.astype(np.int32))[None, :], axis=1)
    second = jnp.sum(match * jnp.asarray(cols_np.astype(np.int32))[None, :], axis=1)
    swapped = jnp.stack([spectra[:, :, 1], -spectra[:, :, 0]], axis=2)
    plain_blocks = spectra.reshape(block_count, BLOCK, width)
    paired = jnp.stack([plain_blocks, swapped.reshape(block_count, BLOCK, width)], axis=1)
    left_blocks = paired[first]
    right_blocks = plain_blocks[second]
    return jnp.einsum(
        "scuw,svw->scuv", left_blocks, right_blocks, preferred_element_type=jnp.float32
    )


def any_sizes(samples, taps, tile_order):
    inputs_here = samples.shape[1]
    sample_count = samples.shape[2]
    tap_count = taps.shape[0]
    fft_size = taps.shape[1]
    frame_count = sample_count // fft_size
    volts = samples.astype(jnp.bfloat16)
    rim_length = (tap_count - 1) * fft_size
    earlier = passed_along(volts[:, :, sample_count - rim_length :], "pair", 1)
    longer = jnp.concatenate([earlier, volts], axis=2).astype(jnp.float32)
    framed = longer.reshape(2, inputs_here, frame_count + tap_count - 1, fft_size)
    weights = taps.astype(jnp.float32)
    filtered = jnp.zeros((2, inputs_here, frame_count, fft_size), jnp.float32)
    for tap_index in range(tap_count):
        filtered = (
            filtered
            + weights[tap_index][None, None, None, :]
            * framed[:, :, tap_index : tap_index + frame_count, :]
        )
    filtered = filtered.astype(jnp.bfloat16)
    left = jnp.concatenate([filtered[0], filtered[1]], axis=-1)
    table = dft_table(fft_size)
    spectra = jnp.einsum("xfm,mck->xfck", left, table, preferred_element_type=jnp.float32)
    chan_size = lax.axis_size("chan")
    group_width = fft_size // chan_size
    spectra = (
        (spectra * 2.0 ** (-14))
        .astype(jnp.bfloat16)
        .reshape(inputs_here, frame_count, 2, chan_size, group_width)
    )
    turned = lax.all_to_all(spectra, "chan", split_axis=3, concat_axis=0, tiled=True)
    turned = turned.reshape(turned.shape[0], frame_count, 2, group_width)
    tile_count = tile_order.shape[0]
    pair_size = lax.axis_size("pair")
    factor = 1.0 / (frame_count * group_width * pair_size)
    summed = lax.psum_scatter(
        tile_products(turned, tile_order, tile_count), "pair", scatter_dimension=0, tiled=True
    )
    return (summed * factor).astype(jnp.bfloat16)[None]


def per_device(samples, taps, tile_order):
    fft_size = taps.shape[1]
    groups = lax.axis_size("chan")
    pair_size = lax.axis_size("pair")
    far = groups // 2
    table = jnp.asarray(grouped_table(fft_size, groups))

    slots = tile_order.shape[0] // pair_size
    def after(value, *others):
        return lax.optimization_barrier((value, *others))[0]

    def to(mask, value):
        return swapped_with(value, "chan", mask)

    def other_core(value):
        return swapped_with(value, "pair", 1)

    def among_near(value):
        halves = [list(range(start, start + far)) for start in range(0, groups, far)]
        return lax.all_to_all(value, "chan", 0, 0, axis_index_groups=halves, tiled=True)

    apart = range(far, groups)
    FIRST, SECOND, THIRD = PLAN
    end = samples.shape[2] // fft_size
    start_a, start_b = end - FIRST, end - FIRST - SECOND
    made_a, (rim_here,) = front(samples, None, taps, table, None, start_a, FIRST, ((FIRST,),) * far + ((),) * far, True)
    a = {mask: to(mask, made_a[mask - far][0]) for mask in apart}
    rim = passed_along(rim_here, "pair", 1)
    sends = ((SECOND,),) * far + ((),) * far
    made_b, _ = front(samples, rim, taps, table, made_a[0][0], start_b, SECOND, sends, False)
    b = {}
    for mask, gate in zip(apart, [a[far], a[far + 1], a[far + 2], a[far + 3]]):
        b[mask] = to(mask, after(made_b[mask - far][0], gate))
    sends = ((THIRD,),) * far + ((THIRD, SECOND, FIRST),) * far
    made_c, (near_c, near_b, near_a) = front(samples, rim, taps, table, made_b[0][0], 0, end, sends, False)
    aa = among_near(near_a)
    bb = among_near(near_b)
    first, second = slot_places(tile_order, groups, slots, made_c[0][0])
    mine = gathered([[(aa, k, 0, FIRST)] for k in range(far)] + [[(a[mask], None, 0, FIRST)] for mask in apart], first)
    other = other_core(mine)
    sums = tiles(first, second, [mine], None, None)
    half_sums = sums
    sums = tiles(first, second, [other], sums, None)
    c = {}
    for mask, gate in zip(apart, [rim, b[far], b[far + 2], b[far + 3]]):
        c[mask] = to(mask, after(made_c[mask - far][0], gate, half_sums) if mask > far else after(made_c[mask - far][0], gate))
    cc = among_near(near_c)
    mine = gathered([[(bb, k, 0, SECOND)] for k in range(far)] + [[(b[mask], None, 0, SECOND)] for mask in apart], sums)
    other = other_core(mine)
    sums = tiles(first, second, [mine], sums, None)
    sums = tiles(first, second, [other], sums, None)
    last = [(cc, k) for k in range(far)] + [(c[mask], None) for mask in apart]
    near_there = other_core(after(cc, sums))
    there = [(near_there, k) for k in range(far)] + [(other_core(after(c[mask], sums)), None) for mask in apart]
    factor = 1.0 / (end * pair_size * (fft_size // groups))
    first, second = slot_places(tile_order, groups, slots, sums)
    sums = tiles(first, second, [last, there], sums, factor)
    return sums.reshape(1, slots, 2, BLOCK, BLOCK)


def chosen(samples, taps, tile_order):
    groups, pair_size = lax.axis_size("chan"), lax.axis_size("pair")
    whole_blocks = samples.shape[1] == BLOCK and taps.shape[1] == groups * LANES
    halves = groups >= 2 and groups & (groups - 1) == 0 and pair_size == 2
    planned = samples.shape[2] == sum(PLAN) * taps.shape[1] and taps.shape[0] - 1 <= PLAN[2]
    if whole_blocks and halves and planned:
        return per_device(samples, taps, tile_order)
    return any_sizes(samples, taps, tile_order)


def solution(mesh):
    in_specs = (P(None, "chan", ("band", "pair")), P(), P())
    out_specs = P(("band", "chan"), "pair", None, None, None)
    return jax.shard_map(chosen, mesh=mesh, in_specs=in_specs, out_specs=out_specs, check_vma=False)
```

```python
import functools
import math

import jax
import jax.numpy as jnp
import ml_dtypes
import numpy as np
from jax import lax
from jax.experimental import pallas as pl
from jax.experimental.pallas import tpu as pltpu
from jax.sharding import PartitionSpec as P

BLOCK = 256
UNROLL = 3
COST = 10**11
LANES = 128
ROWS = 32
SCALE = 2.0**-14
VMEM_LIMIT = 63 * 1024 * 1024

PLAN = (1, 3, 4)


def passed_along(block, axis, distance):
    devices = range(lax.axis_size(axis))
    route = [(i - distance, i) for i in devices if i - distance in devices]
    return lax.ppermute(block, axis, route)


def swapped_with(block, axis, mask):
    return lax.ppermute(block, axis, [(i, i ^ mask) for i in range(lax.axis_size(axis))])


def grouped_table(length, groups):
    index = np.arange(length)
    angle = (index[:, None] * index[None, :] % length).astype(np.float32) * np.float32(2.0 * math.pi / length)
    cosine = np.cos(angle).astype(ml_dtypes.bfloat16).astype(np.float32) * SCALE
    sine = np.sin(angle).astype(ml_dtypes.bfloat16).astype(np.float32) * SCALE
    both = np.stack([cosine, sine], axis=1).reshape(length, 2, groups, length // groups)
    return both.transpose(2, 0, 1, 3).reshape(groups, length, 2 * (length // groups)).astype(ml_dtypes.bfloat16)


def front_kernel(geometry, samples, *refs):
    first, count, sends, with_rim, gated, fft_size, tap_count = geometry
    groups = len(sends)
    reach = tap_count - 1
    early = max(0, reach - first)
    own = count + reach - early
    refs = list(refs)
    rim_in = refs.pop(0) if early else None
    taps, table = refs.pop(0), refs.pop(0)
    if gated:
        refs.pop(0)
    pieces = [[refs.pop(0) for _ in widths] for widths in sends[: groups // 2]]
    near_out = [refs.pop(0) for _ in sends[-1]]
    for j in range(groups // 2, groups):
        pieces.append([out.at[j - groups // 2] for out in near_out])
    rim_out = refs.pop(0) if with_rim else None
    held = refs.pop(0)
    held_rim = refs.pop(0) if early else None
    tables, left, results = refs.pop(0), refs.pop(0), refs.pop(0)
    rim_made = refs.pop(0) if with_rim else None
    in_sems, table_sems, out_sems = refs[:3]
    steps = BLOCK // ROWS
    turns = left.shape[0]
    each, share = steps // turns, BLOCK // turns
    me = lax.axis_index("chan")

    def copies_in(step):
        rows = pl.ds(pl.multiple_of(step * ROWS, ROWS), ROWS)
        lanes = pl.ds((first - reach + early) * fft_size, own * fft_size)
        made = [pltpu.make_async_copy(samples.at[:, rows, lanes], held.at[:, rows, :], in_sems.at[0, step])]
        if early:
            lanes = pl.ds((reach - early) * fft_size, early * fft_size)
            made.append(pltpu.make_async_copy(rim_in.at[:, rows, lanes], held_rim.at[:, rows, :], in_sems.at[1, step]))
        return made

    def copy_table(j):
        group = me ^ (j + groups // 2) if j < groups // 2 else me - lax.rem(me, groups // 2) + (j - groups // 2)
        return pltpu.make_async_copy(table.at[group], tables.at[j], table_sems.at[j])

    def copies_out(j):
        made, f = [], 0
        for w, width in enumerate(sends[j]):
            part = results.at[j, :, f * BLOCK : (f + width) * BLOCK]
            made.append(pltpu.make_async_copy(part, pieces[j][w], out_sems.at[j, w]))
            f += width
        return made

    used = [j for j in range(groups) if sends[j]]
    for step in range(steps):
        for copy in copies_in(step):
            copy.start()
    for j in used:
        copy_table(j).start()

    def filter_rows(turn, step, carry):
        for copy in copies_in(step):
            copy.wait()
        rows = pl.ds(pl.multiple_of(step * ROWS, ROWS), ROWS)
        for part in range(2):
            for start in range(0, fft_size, LANES):
                values = []
                for k in range(early):
                    lanes = slice(k * fft_size + start, k * fft_size + start + LANES)
                    values.append(held_rim[part, rows, lanes].astype(jnp.float32))
                for k in range(own):
                    lanes = slice(k * fft_size + start, k * fft_size + start + LANES)
                    values.append(held[part, rows, lanes].astype(jnp.float32))
                lanes = slice(start, start + LANES)
                weights = [taps[t : t + 1, lanes].astype(jnp.float32) for t in range(tap_count)]
                for f in range(count):
                    total = weights[0] * values[f]
                    for t in range(1, tap_count):
                        total = total + weights[t] * values[f + t]
                    at = pl.ds(pl.multiple_of(f * share + (step - turn * each) * ROWS, ROWS), ROWS)
                    left[turn, part, at, lanes] = total.astype(jnp.bfloat16)
                if with_rim:
                    for t in range(reach):
                        lanes = slice(t * fft_size + start, t * fft_size + start + LANES)
                        rim_made[part, rows, lanes] = values[count + t].astype(jnp.bfloat16)
        return carry


    def transform(j, frames, turn):
        if turn == 0:
            pltpu.make_async_copy(table.at[0], tables.at[j], table_sems.at[j]).wait()

        rows = frames * share
        product = [
            jnp.dot(left[turn, part, :rows, :], tables[j], preferred_element_type=jnp.float32) for part in range(2)
        ]
        real = (product[0][:, :LANES] + product[1][:, LANES:]).astype(jnp.bfloat16)
        imag = (product[1][:, :LANES] - product[0][:, LANES:]).astype(jnp.bfloat16)
        at = slice(turn * share, (turn + 1) * share)
        for f in range(frames):
            results[j, at, f * BLOCK : f * BLOCK + LANES] = real[f * share : (f + 1) * share]
            results[j, at, f * BLOCK + LANES : (f + 1) * BLOCK] = imag[f * share : (f + 1) * share]
        if turn + 1 < turns:
            return
        for k in used:

            @pl.when(j == k)
            def _():
                for copy in copies_out(k):
                    copy.start()

    for turn in range(turns):
        lax.fori_loop(turn * each, (turn + 1) * each, functools.partial(filter_rows, turn), 0)
        if with_rim and turn + 1 == turns:
            rim_copy = pltpu.make_async_copy(rim_made, rim_out, in_sems.at[1, 0])
            rim_copy.start()
        begin = used[0]
        while begin <= used[-1]:
            end = begin
            while end <= used[-1] and sum(sends[end]) == sum(sends[begin]):
                end += 1

            def several(j, carry, frames=sum(sends[begin]), turn=turn):
                transform(j, frames, turn)
                return carry

            lax.fori_loop(begin, end, several, 0, unroll=2)
            begin = end
    if with_rim:
        rim_copy.wait()
    for j in used:
        for copy in copies_out(j):
            copy.wait()


def front(samples, rim, taps, table, gate, first, count, sends, with_rim):
    fft_size = taps.shape[1]
    tap_count = taps.shape[0]
    reach = tap_count - 1
    groups, depth, columns = len(sends), table.shape[1], table.shape[2]
    early = max(0, reach - first)
    own = count + reach - early
    turns = 1
    anywhere = pl.BlockSpec(memory_space=pl.ANY)
    vmem = pl.BlockSpec(memory_space=pltpu.VMEM)
    operands = [samples] + ([rim] if early else []) + [taps, table] + ([] if gate is None else [gate])
    in_specs = [anywhere] + ([anywhere] if early else []) + [vmem, anywhere] + ([] if gate is None else [anywhere])
    out_shape = []
    for widths in sends[: groups // 2]:
        for width in widths:
            out_shape.append(jax.ShapeDtypeStruct((BLOCK, width * columns), jnp.bfloat16))
    for width in sends[-1]:
        out_shape.append(jax.ShapeDtypeStruct((groups // 2, BLOCK, width * columns), jnp.bfloat16))
    scratch = [pltpu.VMEM((2, BLOCK, own * fft_size), jnp.int32)]
    if early:
        scratch.append(pltpu.VMEM((2, BLOCK, early * fft_size), jnp.bfloat16))
    scratch += [
        pltpu.VMEM((groups, depth, columns), jnp.bfloat16),
        pltpu.VMEM((turns, 2, count * BLOCK // turns, depth), jnp.bfloat16),
        pltpu.VMEM((groups, BLOCK, count * columns), jnp.bfloat16),
    ]
    if with_rim:
        out_shape.append(jax.ShapeDtypeStruct((2, BLOCK, reach * fft_size), jnp.bfloat16))
        scratch.append(pltpu.VMEM((2, BLOCK, reach * fft_size), jnp.bfloat16))
    scratch += [
        pltpu.SemaphoreType.DMA((2, BLOCK // ROWS)),
        pltpu.SemaphoreType.DMA((groups,)),
        pltpu.SemaphoreType.DMA((groups, max(len(widths) for widths in sends))),
    ]
    geometry = (first, count, sends, with_rim, gate is not None, fft_size, tap_count)
    results = list(
        pl.pallas_call(
            functools.partial(front_kernel, geometry),
            in_specs=in_specs,
            out_specs=[anywhere] * len(out_shape),
            out_shape=out_shape,
            scratch_shapes=scratch,
            compiler_params=pltpu.CompilerParams(vmem_limit_bytes=VMEM_LIMIT),
            cost_estimate=pl.CostEstimate(flops=COST, bytes_accessed=1, transcendentals=0),
        )(*operands)
    )
    pieces = [[results.pop(0) for _ in widths] for widths in sends[: groups // 2]]
    return pieces, results


def gather_kernel(layout, *refs):
    parts, out, held, in_sems, out_sems = refs[:-4], *refs[-4:]
    copies, sends = [], []
    for d, places in enumerate(layout):
        f = 0
        for w, (number, at, start, width) in enumerate(places):
            source = parts[number] if at is None else parts[number].at[at]
            source = source.at[:, start * BLOCK : (start + width) * BLOCK]
            target = held.at[d, :, f * BLOCK : (f + width) * BLOCK]
            copies.append((d, pltpu.make_async_copy(source, target, in_sems.at[d, w])))
            f += width
        sends.append(pltpu.make_async_copy(held.at[d], out.at[d], out_sems.at[d]))
    for _, copy in copies:
        copy.start()
    for d, send in enumerate(sends):
        for owner, copy in copies:
            if owner == d:
                copy.wait()
        send.start()
    for send in sends:
        send.wait()


def gathered(blocks, after):
    operands, layout = [], []
    for block in blocks:
        places = []
        for array, at, start, width in block:
            places.append((len(operands), at, start, width))
            operands.append(array)
        layout.append(tuple(places))
    frames = sum(place[3] for place in layout[0])
    shape = (len(blocks), BLOCK, frames * BLOCK)
    operands += [] if after is None else [after]
    return pl.pallas_call(
        functools.partial(gather_kernel, tuple(layout)),
        in_specs=[pl.BlockSpec(memory_space=pl.ANY)] * len(operands),
        out_specs=pl.BlockSpec(memory_space=pl.ANY),
        out_shape=jax.ShapeDtypeStruct(shape, jnp.bfloat16),
        scratch_shapes=[
            pltpu.VMEM(shape, jnp.bfloat16),
            pltpu.SemaphoreType.DMA((len(blocks), max(len(places) for places in layout))),
            pltpu.SemaphoreType.DMA((len(blocks),)),
        ],
        compiler_params=pltpu.CompilerParams(vmem_limit_bytes=VMEM_LIMIT),
        cost_estimate=pl.CostEstimate(flops=1, bytes_accessed=1, transcendentals=0),
    )(*operands)


def tile_kernel(geometry, first, second, *refs):
    layout, inputs, has_sums, factor = geometry
    count = len(layout)
    arrays = refs[:inputs]
    sums = refs[inputs] if has_sums else None
    refs = refs[inputs + has_sums :]
    out, held, totals = refs[0], refs[1 : 1 + count], refs[1 + count]
    finished = refs[2 + count]
    partial = refs[3 + count] if count == 2 else None
    block_sems, sum_sems, out_sems = refs[-3:]
    slots = totals.shape[0]
    copies = []
    for k, places in enumerate(layout):
        copies.append([])
        for d, (number, at) in enumerate(places):
            source = arrays[number] if at is None else arrays[number].at[at]
            copies[k].append(pltpu.make_async_copy(source, held[k].at[d], block_sems.at[k, d]))
    for copy in copies[0]:
        copy.start()

    def copy_in(slot):
        return pltpu.make_async_copy(sums.at[slot], totals.at[slot], sum_sems.at[slot])

    def copy_out(slot):
        return pltpu.make_async_copy(finished.at[slot], out.at[slot], out_sems.at[slot])

    stage = -(-slots // (2 if count == 2 else 3))
    stages = [range(start, min(start + stage, slots)) for start in range(0, slots, stage)]
    if has_sums and count == 1:
        for slot in stages[0]:
            copy_in(slot).start()
    for copy in copies[0]:
        copy.wait()

    def term_of(block, slot):
        left, right = block[first[slot]], block[second[slot]]
        turned = []
        for start in range(0, left.shape[1], 2 * LANES):
            turned += [left[:, start + LANES : start + 2 * LANES], -left[:, start : start + LANES]]
        both = jnp.concatenate([left, jnp.concatenate(turned, axis=1)], axis=0)
        return lax.dot_general(both, right, (((1,), (1,)), ((), ())), preferred_element_type=jnp.float32)

    def begin(slot, carry):
        partial[slot] = term_of(held[0], slot)
        return carry

    if count == 2:
        for copy in copies[1]:
            copy.start()
        for slot in range(slots):
            copy_in(slot).start()
        lax.fori_loop(0, slots, begin, 0, unroll=9)
        for copy in copies[1]:
            copy.wait()

    def correlate(slot, carry):
        total = term_of(held[-1], slot)
        if count == 2:
            total = total + partial[slot]
        if has_sums:
            total = total + totals[slot]
        if factor is not None:
            total = total * factor
        finished[slot] = total.astype(finished.dtype)
        copy_out(slot).start()
        return carry

    for number, several in enumerate(stages):
        if has_sums:
            for slot in several:
                copy_in(slot).wait()
            for slot in stages[number + 1] if number + 1 < len(stages) and count == 1 else ():
                copy_in(slot).start()
        lax.fori_loop(several.start, several.stop, correlate, 0, unroll=UNROLL if factor is None else 9)
    for slot in range(slots):
        copy_out(slot).wait()


def tiles(first, second, blocks, sums, factor):
    slots = first.shape[0]
    anywhere = pl.BlockSpec(memory_space=pl.ANY)
    smem = pl.BlockSpec(memory_space=pltpu.SMEM)
    operands, layout = [], []
    for places in blocks:
        if not isinstance(places, list):
            places = [(places, d) for d in range(places.shape[0])]
        numbered = []
        for array, at in places:
            number = next((n for n, known in enumerate(operands) if known is array), len(operands))
            operands += [array] if number == len(operands) else []
            numbered.append((number, at))
        layout.append(tuple(numbered))
    inputs = len(operands)
    operands += [] if sums is None else [sums]
    shape = (slots, 2 * BLOCK, BLOCK)
    kind = jnp.float32 if factor is None else jnp.bfloat16
    scratch = [pltpu.VMEM((len(places),) + operands[places[0][0]].shape[-2:], jnp.bfloat16) for places in layout] + [pltpu.VMEM(shape, jnp.float32), pltpu.VMEM(shape, kind)]
    scratch += [pltpu.VMEM(shape, jnp.float32)] if len(blocks) == 2 else []
    scratch += [
        pltpu.SemaphoreType.DMA((len(layout), len(layout[0]))),
        pltpu.SemaphoreType.DMA((slots,)),
        pltpu.SemaphoreType.DMA((slots,)),
    ]
    return pl.pallas_call(
        functools.partial(tile_kernel, (tuple(layout), inputs, sums is not None, factor)),
        in_specs=[smem, smem] + [anywhere] * len(operands),
        out_specs=anywhere,
        out_shape=jax.ShapeDtypeStruct(shape, kind),
        scratch_shapes=scratch,
        compiler_params=pltpu.CompilerParams(vmem_limit_bytes=VMEM_LIMIT),
        cost_estimate=pl.CostEstimate(flops=COST, bytes_accessed=1, transcendentals=0),
    )(first, second, *operands)


def slots_kernel(groups, tile_order, gate, first, second):
    me, core = lax.axis_index("chan"), lax.axis_index("pair")
    slots, far = first.shape[0], groups // 2
    starts = [a * groups - a * (a - 1) // 2 for a in range(groups)]
    my_half = me >= far

    def place(block):
        return jnp.where((block >= far) == my_half, lax.rem(block, far), block ^ me)

    def one(slot, carry):
        tile = tile_order[core * slots + slot]
        row, begin = jnp.int32(0), jnp.int32(0)
        for a in range(1, groups):
            row = row + jnp.where(tile >= starts[a], 1, 0)
            begin = jnp.where(tile >= starts[a], starts[a], begin)
        first[slot] = place(row)
        second[slot] = place(tile - begin + row)
        return carry

    lax.fori_loop(0, slots, one, 0)


def slot_places(tile_order, groups, slots, gate):
    smem = pl.BlockSpec(memory_space=pltpu.SMEM)
    places = jax.ShapeDtypeStruct((slots,), jnp.int32)
    return pl.pallas_call(
        functools.partial(slots_kernel, groups),
        in_specs=[smem, pl.BlockSpec(memory_space=pl.ANY)],
        out_specs=[smem, smem],
        out_shape=[places, places],
        cost_estimate=pl.CostEstimate(flops=COST, bytes_accessed=1, transcendentals=0),
    )(tile_order, gate)


def dft_table(length):
    index = jnp.arange(length, dtype=jnp.int32)
    phase = index[:, None] * index[None, :] % length
    angle = phase.astype(jnp.float32) * (2.0 * math.pi / length)
    cosine = jnp.cos(angle)
    sine = jnp.sin(angle)
    upper = jnp.stack([cosine, -sine], axis=1)
    lower = jnp.stack([sine, cosine], axis=1)
    return jnp.concatenate([upper, lower], axis=0).astype(jnp.bfloat16)


def tile_products(spectra, slots, tile_count):
    input_count = spectra.shape[0]
    block_count = input_count // BLOCK
    width = spectra.shape[1] * spectra.shape[2] * spectra.shape[3]
    rows_np, cols_np = np.triu_indices(block_count)
    numbers = jnp.arange(tile_count, dtype=jnp.int32)
    match = (slots[:, None] == numbers[None, :]).astype(jnp.int32)
    first = jnp.sum(match * jnp.asarray(rows_np.astype(np.int32))[None, :], axis=1)
    second = jnp.sum(match * jnp.asarray(cols_np.astype(np.int32))[None, :], axis=1)
    swapped = jnp.stack([spectra[:, :, 1], -spectra[:, :, 0]], axis=2)
    plain_blocks = spectra.reshape(block_count, BLOCK, width)
    paired = jnp.stack([plain_blocks, swapped.reshape(block_count, BLOCK, width)], axis=1)
    left_blocks = paired[first]
    right_blocks = plain_blocks[second]
    return jnp.einsum(
        "scuw,svw->scuv", left_blocks, right_blocks, preferred_element_type=jnp.float32
    )


def any_sizes(samples, taps, tile_order):
    inputs_here = samples.shape[1]
    sample_count = samples.shape[2]
    tap_count = taps.shape[0]
    fft_size = taps.shape[1]
    frame_count = sample_count // fft_size
    volts = samples.astype(jnp.bfloat16)
    rim_length = (tap_count - 1) * fft_size
    earlier = passed_along(volts[:, :, sample_count - rim_length :], "pair", 1)
    longer = jnp.concatenate([earlier, volts], axis=2).astype(jnp.float32)
    framed = longer.reshape(2, inputs_here, frame_count + tap_count - 1, fft_size)
    weights = taps.astype(jnp.float32)
    filtered = jnp.zeros((2, inputs_here, frame_count, fft_size), jnp.float32)
    for tap_index in range(tap_count):
        filtered = (
            filtered
            + weights[tap_index][None, None, None, :]
            * framed[:, :, tap_index : tap_index + frame_count, :]
        )
    filtered = filtered.astype(jnp.bfloat16)
    left = jnp.concatenate([filtered[0], filtered[1]], axis=-1)
    table = dft_table(fft_size)
    spectra = jnp.einsum("xfm,mck->xfck", left, table, preferred_element_type=jnp.float32)
    chan_size = lax.axis_size("chan")
    group_width = fft_size // chan_size
    spectra = (
        (spectra * 2.0 ** (-14))
        .astype(jnp.bfloat16)
        .reshape(inputs_here, frame_count, 2, chan_size, group_width)
    )
    turned = lax.all_to_all(spectra, "chan", split_axis=3, concat_axis=0, tiled=True)
    turned = turned.reshape(turned.shape[0], frame_count, 2, group_width)
    tile_count = tile_order.shape[0]
    pair_size = lax.axis_size("pair")
    factor = 1.0 / (frame_count * group_width * pair_size)
    summed = lax.psum_scatter(
        tile_products(turned, tile_order, tile_count), "pair", scatter_dimension=0, tiled=True
    )
    return (summed * factor).astype(jnp.bfloat16)[None]


def per_device(samples, taps, tile_order):
    fft_size = taps.shape[1]
    groups = lax.axis_size("chan")
    pair_size = lax.axis_size("pair")
    far = groups // 2
    table = jnp.asarray(grouped_table(fft_size, groups))

    slots = tile_order.shape[0] // pair_size
    def after(value, *others):
        return lax.optimization_barrier((value, *others))[0]

    def to(mask, value):
        return swapped_with(value, "chan", mask)

    def other_core(value):
        return swapped_with(value, "pair", 1)

    def among_near(value):
        halves = [list(range(start, start + far)) for start in range(0, groups, far)]
        return lax.all_to_all(value, "chan", 0, 0, axis_index_groups=halves, tiled=True)

    apart = range(far, groups)
    FIRST, SECOND, THIRD = PLAN
    end = samples.shape[2] // fft_size
    start_a, start_b = end - FIRST, end - FIRST - SECOND
    made_a, (rim_here,) = front(samples, None, taps, table, None, start_a, FIRST, ((FIRST,),) * far + ((),) * far, True)
    a = {mask: to(mask, made_a[mask - far][0]) for mask in apart}
    rim = passed_along(rim_here, "pair", 1)
    sends = ((SECOND,),) * far + ((),) * far
    made_b, _ = front(samples, rim, taps, table, made_a[0][0], start_b, SECOND, sends, False)
    b = {}
    for mask, gate in zip(apart, [a[far], a[far + 1], a[far + 2], a[far + 3]]):
        b[mask] = to(mask, after(made_b[mask - far][0], gate))
    sends = ((THIRD,),) * far + ((THIRD, SECOND, FIRST),) * far
    made_c, (near_c, near_b, near_a) = front(samples, rim, taps, table, made_b[0][0], 0, end, sends, False)
    aa = among_near(near_a)
    bb = among_near(near_b)
    first, second = slot_places(tile_order, groups, slots, made_c[0][0])
    mine = gathered([[(aa, k, 0, FIRST)] for k in range(far)] + [[(a[mask], None, 0, FIRST)] for mask in apart], first)
    other = other_core(mine)
    sums = tiles(first, second, [mine], None, None)
    half_sums = sums
    sums = tiles(first, second, [other], sums, None)
    c = {}
    for mask, gate in zip(apart, [rim, b[far], b[far + 2], b[far + 3]]):
        c[mask] = to(mask, after(made_c[mask - far][0], gate, half_sums) if mask > far else after(made_c[mask - far][0], gate))
    cc = among_near(near_c)
    mine = gathered([[(bb, k, 0, SECOND)] for k in range(far)] + [[(b[mask], None, 0, SECOND)] for mask in apart], sums)
    other = other_core(mine)
    sums = tiles(first, second, [mine], sums, None)
    sums = tiles(first, second, [other], sums, None)
    last = [(cc, k) for k in range(far)] + [(c[mask], None) for mask in apart]
    near_there = other_core(after(cc, sums))
    there = [(near_there, k) for k in range(far)] + [(other_core(after(c[mask], sums)), None) for mask in apart]
    factor = 1.0 / (end * pair_size * (fft_size // groups))
    first, second = slot_places(tile_order, groups, slots, sums)
    sums = tiles(first, second, [last, there], sums, factor)
    return sums.reshape(1, slots, 2, BLOCK, BLOCK)


def chosen(samples, taps, tile_order):
    groups, pair_size = lax.axis_size("chan"), lax.axis_size("pair")
    whole_blocks = samples.shape[1] == BLOCK and taps.shape[1] == groups * LANES
    halves = groups >= 2 and groups & (groups - 1) == 0 and pair_size == 2
    planned = samples.shape[2] == sum(PLAN) * taps.shape[1] and taps.shape[0] - 1 <= PLAN[2]
    if whole_blocks and halves and planned:
        return per_device(samples, taps, tile_order)
    return any_sizes(samples, taps, tile_order)


def solution(mesh):
    in_specs = (P(None, "chan", ("band", "pair")), P(), P())
    out_specs = P(("band", "chan"), "pair", None, None, None)
    return jax.shard_map(chosen, mesh=mesh, in_specs=in_specs, out_specs=out_specs, check_vma=False)
```
